32 devices in a mesh: groups: 2 (over x), pool: 16 (over z, y, core).
Axes of the slice: x: 2, y: 2, z: 4, core: 2. Of those that a mesh axis runs over, the one named last changes fastest.
Arguments:
- queries: bfloat16 [1024, 16384], P(None, ('groups', 'pool')), parts along dimension 1, may hold values from -80 to 80
- stretch_keys: bfloat16 [16384, 128], P(('groups', 'pool')), parts along dimension 0, may hold values from -6 to 6
- stretch_values: bfloat16 [16384, 128], P(('groups', 'pool')), parts along dimension 0, may hold values from -6 to 6
- pool_keys: bfloat16 [96, 256, 128], P(('groups', 'pool')), parts along dimension 0, may hold values from -8 to 8
- pool_values: bfloat16 [96, 256, 128], P(('groups', 'pool')), parts along dimension 0, may hold values from -6 to 6
- page_counts: int32 [4], P('groups'), parts along dimension 0, may hold values from 1 to 11, as said below
- page_table: int32 [4, 4, 11], P('groups'), parts along dimension 0, may hold values from -1 to 47, as said below
Outputs:
- attended: bfloat16 [1024, 16384], P(None, ('groups', 'pool')), parts along dimension 1
The draws below stay inside these ranges and needn't reach their ends.
There are 2 independent parts, one for each index of `groups`. The reference program is written for one: setup_inputs(seed, part) draws one part's arguments, and reference() takes and returns one part's arrays. A program takes and returns all parts, laid end to end along the dimension named above; each array names one. Nothing has to cross between parts.
Inputs may be any that keep to these rules, and one draw needn't show every extreme that they name: `page_counts`: the counts sum to 12; the largest is exactly 11. `page_table`: entry [r, g, j] with j < page_counts[r] is the slot of pool_keys and pool_values holding page j of request r for key head g; slot s lies on device s // 3 of the pool axis. Other entries are -1. Every slot is named exactly once. No device holds two slots named by the same r and g.
All inputs are finite; a program needn't handle non-finite values.
Results may differ from the reference program's by a relative error of at most 0.0055.
Values may be sent and summed in bfloat16 or wider, within the bound.
No kernel may reach another device: no remote copies, remote signals or barrier semaphores. Data moves between devices by JAX's collectives and lax.ppermute only.
A program may use at most 64 MiB of HBM per device.

```python
import math
import jax
import jax.numpy as jnp
from jax import lax

HD = 128
QH = 32
KVH = 4
PAGE = 256
STRETCH = 1024
SLOTS_DEV = 3
REQS = 2
MEANP = 6
MAXP = 11
SLOTS = 48
N_POOL = 16


def layout(key):
    key_long, key_cells, key_devices, key_shift = jax.random.split(key, 4)
    longest = jax.random.randint(key_long, (), 0, REQS)
    extra_units = REQS * MEANP - MAXP - (REQS - 1)
    cell_total = (REQS - 1) * (MAXP - 1)
    order = jax.random.permutation(key_cells, cell_total)
    taken = (order < extra_units).astype(jnp.int32)
    owners = jnp.arange(cell_total) // (MAXP - 1)
    extra = jnp.sum(jnp.where(owners[None, :] == jnp.arange(REQS - 1)[:, None], taken[None, :], 0), axis=1)
    others = 1 + extra
    requests = jnp.arange(REQS)
    shifted = jnp.clip(requests - (requests > longest).astype(jnp.int32), 0, REQS - 2)
    counts = jnp.where(requests == longest, MAXP, others[shifted])
    sizes = jnp.repeat(counts, KVH)
    starts = jnp.cumsum(sizes) - sizes
    pages = jnp.arange(MAXP)
    position = starts[:, None] + pages[None, :]
    devices = jax.random.permutation(key_devices, N_POOL)
    shifts = jax.random.randint(key_shift, (N_POOL,), 0, SLOTS_DEV)
    device_of = devices[position % N_POOL]
    slot_of = (position // N_POOL + shifts[device_of]) % SLOTS_DEV
    table = jnp.where(pages[None, :] < sizes[:, None], device_of * SLOTS_DEV + slot_of, -1)
    return (counts.astype(jnp.int32), table.reshape(REQS, KVH, MAXP).astype(jnp.int32))


def draw_page_counts(key, part):
    counts, table = layout(key)
    return counts


def draw_page_table(key, part):
    counts, table = layout(key)
    return table


def draw_queries(key, part):
    key = jax.random.fold_in(key, 1)
    first_key = jax.random.fold_in(key, 0)
    shape_three = (STRETCH, REQS * QH, HD)
    values = jax.random.normal(first_key, shape_three, jnp.float32)
    return values.reshape(STRETCH, REQS * QH * HD).astype(jnp.bfloat16)


def draw_pool_keys(key, part):
    key = jax.random.fold_in(key, 2)
    values = jax.random.normal(key, (SLOTS, PAGE, HD), jnp.float32)
    return values.astype(jnp.bfloat16)


def shard_levels(key, shape, shards, smallest, largest):
    level, own = 1.0, jax.random.fold_in(key, 6)
    for axis_at, parts in shards:
        steps = jnp.exp(jax.random.uniform(jax.random.fold_in(own, axis_at), (parts,), jnp.float32, smallest / len(shards), largest / len(shards)))
        level = level * jnp.repeat(steps, shape[axis_at] // parts).reshape([-1 if axis == axis_at else 1 for axis in range(len(shape))])
    return level


def bell_draw(own_key, dims, width, reach, cuts=(), dtype=jnp.bfloat16):
    values = jax.random.normal(own_key, dims, jnp.float32) * width
    if len(cuts) > 0:
        values = shard_levels(own_key, dims, cuts, -0.22, 0.18) * values
    return jnp.clip(values, min=-reach, max=reach).astype(dtype)


def setup_inputs(seed: int = 0, part: int = 0) -> dict:
    key_of = jax.random.split(jax.random.key(seed), 8)
    part_keys = jax.random.split(jax.random.fold_in(key_of[7], part), 8)
    queries = draw_queries(jax.random.fold_in(jax.random.fold_in(key_of[7], part), 71), part)
    stretch_keys = bell_draw(part_keys[1], (REQS * KVH * STRETCH, HD), 1.0, 6.0, ((0, 16),))
    stretch_values = bell_draw(part_keys[2], (REQS * KVH * STRETCH, HD), 1.0, 6.0, ((0, 16),))
    pool_keys = draw_pool_keys(jax.random.fold_in(jax.random.fold_in(key_of[7], part), 71), part)
    pool_values = bell_draw(part_keys[4], (SLOTS, PAGE, HD), 1.0, 6.0, ((0, 16),))
    page_counts = draw_page_counts(jax.random.fold_in(jax.random.fold_in(key_of[7], part), 71), part)
    page_table = draw_page_table(jax.random.fold_in(jax.random.fold_in(key_of[7], part), 71), part)
    return {"queries": queries, "stretch_keys": stretch_keys, "stretch_values": stretch_values, "pool_keys": pool_keys, "pool_values": pool_values, "page_counts": page_counts, "page_table": page_table}


def reference(queries, stretch_keys, stretch_values, pool_keys, pool_values, page_counts, page_table):
    per_group = QH // KVH
    query_all = queries.reshape(STRETCH, REQS, KVH, per_group, HD)
    new_keys = stretch_keys.reshape(REQS, KVH, STRETCH, HD)
    new_values = stretch_values.reshape(REQS, KVH, STRETCH, HD)
    positions = jnp.arange(STRETCH)
    causal = positions[None, :] <= positions[:, None]
    score_scale = 1.0 / math.sqrt(HD)

    def one_pair(pair_index):
        request = pair_index // KVH
        kv_head = pair_index % KVH
        slot_row = page_table[request, kv_head]
        slot_ids = jnp.maximum(slot_row, 0)
        page_keys = pool_keys[slot_ids].reshape(MAXP * PAGE, HD)
        page_values = pool_values[slot_ids].reshape(MAXP * PAGE, HD)
        live_keys = jnp.repeat(jnp.arange(MAXP) < page_counts[request], PAGE)
        all_keys = jnp.concatenate([page_keys, new_keys[request, kv_head]], axis=0)
        all_values = jnp.concatenate([page_values, new_values[request, kv_head]], axis=0)
        visible = jnp.concatenate([jnp.broadcast_to(live_keys[None, :], (STRETCH, MAXP * PAGE)), causal], axis=1)
        pair_queries = query_all[:, request, kv_head]

        def one_head(head_index):
            one_query = lax.dynamic_index_in_dim(pair_queries, head_index, 1, keepdims=False)
            scores = jnp.dot(one_query, all_keys.T, preferred_element_type=jnp.float32) * score_scale
            scores = jnp.where(visible, scores, -jnp.inf)
            row_max = lax.optimization_barrier(jnp.max(scores, axis=1, keepdims=True))
            weights = jnp.exp(scores - row_max)
            totals = lax.optimization_barrier(jnp.sum(weights, axis=1))
            mixed = jnp.dot(weights.astype(jnp.bfloat16), all_values, preferred_element_type=jnp.float32)
            return (mixed / totals[:, None]).astype(jnp.bfloat16)
        return lax.map(one_head, jnp.arange(per_group))
    result = lax.map(one_pair, jnp.arange(REQS * KVH))
    result = result.reshape(REQS, KVH, per_group, STRETCH, HD).transpose(3, 0, 1, 2, 4)
    return result.reshape(STRETCH, REQS * QH * HD)
```

```python
import functools
import math

import jax
import jax.numpy as jnp
from jax import lax
from jax.experimental import pallas as pl
from jax.experimental.pallas import tpu as pltpu
from jax.sharding import PartitionSpec as P

HD = 128
QH = 32
KVH = 4
PAGE = 256
STRETCH = 1024
SLOTS_DEV = 3
CORES = 2
TILE = 256
VMEM_BYTES = 24 * 2**20
EXP2_SCALE = math.log2(math.e) / math.sqrt(HD)
ROW_BY_ROW = (((1,), (1,)), ((), ()))

SMEM = pl.BlockSpec(memory_space=pltpu.SMEM)
ANY = pl.BlockSpec(memory_space=pl.ANY)


def swapped(value, axis, mask):
    pairs = [(source, source ^ mask) for source in range(lax.axis_size(axis))]
    return lax.ppermute(value, axis, pairs)


def pick_kernel(offsets, own_ref, table_ref, keys_ref, values_ref, *refs):
    outs, sem = refs[:-1], refs[-1]
    own = own_ref[0]
    first = own * SLOTS_DEV
    depth = table_ref.shape[1]
    copies = []
    for at, offset in enumerate(offsets):
        row = jnp.bitwise_xor(own // CORES, offset)

        def look(page, slot, row=row):
            there = table_ref[row, page] - first
            return jnp.where((there >= 0) & (there < SLOTS_DEV), there, slot)

        slot = lax.fori_loop(0, depth, look, 0, unroll=True)
        for side, source in enumerate((keys_ref, values_ref)):
            copy = pltpu.make_async_copy(source.at[slot], outs[at].at[side], sem.at[at, side])
            copy.start()
            copies.append(copy)
    for copy in copies:
        copy.wait()


def pick(own, table, keys, values, offsets):
    return pl.pallas_call(
        functools.partial(pick_kernel, offsets),
        out_shape=[jax.ShapeDtypeStruct((2, PAGE, HD), keys.dtype)] * len(offsets),
        in_specs=[SMEM, SMEM, ANY, ANY],
        out_specs=[ANY] * len(offsets),
        scratch_shapes=[pltpu.SemaphoreType.DMA((len(offsets), 2))],
        compiler_params=pltpu.CompilerParams(vmem_limit_bytes=VMEM_BYTES),
        name="pick",
    )(own, table, keys, values)


def online(scores, values, old_max, old_totals, old_acc):
    width = scores.shape[1] // HD
    peak = jnp.max(scores, axis=1, keepdims=True)
    new_max = jnp.broadcast_to(peak, (scores.shape[0], HD))
    if old_max is not None:
        new_max = jnp.maximum(old_max, new_max)
    weights = jnp.exp2((scores - jnp.concatenate([new_max] * width, 1)) * EXP2_SCALE)
    totals = weights[:, :HD]
    for part in range(1, width):
        totals = totals + weights[:, part * HD : (part + 1) * HD]
    acc = jnp.dot(weights.astype(jnp.bfloat16), values, preferred_element_type=jnp.float32)
    if old_max is not None:
        rescale = jnp.exp2((old_max - new_max) * EXP2_SCALE)
        totals = old_totals * rescale + totals
        acc = old_acc * rescale + acc
    return new_max, totals, acc


def score(query, keys):
    return lax.dot_general(query, keys, ROW_BY_ROW, preferred_element_type=jnp.float32)


def stretch_kernel(own_ref, q_ref, k_ref, k2_ref, v_ref, v2_ref, m_ref, l_ref, a_ref, ks, vs, sem):
    @pl.when(pl.program_id(0) == 0)
    def _():
        half = own_ref[0] % CORES
        rows = k_ref.shape[0]
        copies = []
        for at, (source, target) in enumerate(((k_ref, ks), (k2_ref, ks), (v_ref, vs), (v2_ref, vs))):
            place = half if at % 2 == 0 else 1 - half
            start = pl.multiple_of(place * rows, rows)
            copies.append(pltpu.make_async_copy(source, target.at[pl.ds(start, rows)], sem.at[at]))
            copies[-1].start()
        for copy in copies:
            copy.wait()

    tiles = STRETCH // TILE
    row = lax.broadcasted_iota(jnp.int32, (TILE, TILE), 0)
    column = lax.broadcasted_iota(jnp.int32, (TILE, TILE), 1)

    def scores_of(tile):
        here = slice(tile * TILE, (tile + 1) * TILE)
        scores = score(q_ref[here, :], ks[: (tile + 1) * TILE])
        last = jnp.where(column <= row, scores[:, tile * TILE :], -jnp.inf)
        if tile == 0:
            return last
        return jnp.concatenate([scores[:, : tile * TILE], last], 1)

    order = list(range(tiles))[::-1]
    ahead = scores_of(order[0])
    for at, tile in enumerate(order):
        scores = ahead
        if at + 1 < tiles:
            ahead = scores_of(order[at + 1])
        here = slice(tile * TILE, (tile + 1) * TILE)
        m, l, a = online(scores, vs[: (tile + 1) * TILE], None, None, None)
        m_ref[0, here, :] = m
        l_ref[0, here, :] = l
        a_ref[0, here, :] = a


def pages_kernel(
    low, high, final, own_ref, table_ref, counts_ref, q_ref, near_ref, far_ref, m_in, l_in, a_in, *refs
):
    if final:
        o_ref, ks, vs, fill, m_ref, l_ref, a_ref, sem = refs
    else:
        m_ref, l_ref, a_ref, ks, vs, fill, sem = refs
    own = own_ref[0]
    chip = own // CORES
    core = own % CORES

    def copies(page):
        slot = jnp.maximum(table_ref[chip, page], 0)
        device = slot // SLOTS_DEV
        offset = jnp.bitwise_xor(device // CORES, chip)
        inside = (table_ref[chip, page] >= 0) & (offset >= low) & (offset < high)
        return inside, device % CORES == core, jnp.clip(offset - low, 0, high - low - 1)

    @pl.when(pl.program_id(0) == 0)
    def _():
        depth = table_ref.shape[1]

        def begin(page, filled):
            inside, mine, at = copies(page)

            @pl.when(inside & mine)
            def _():
                pltpu.make_async_copy(near_ref.at[at, 0], ks.at[filled], sem.at[filled, 0]).start()
                pltpu.make_async_copy(near_ref.at[at, 1], vs.at[filled], sem.at[filled, 1]).start()

            @pl.when(inside & jnp.logical_not(mine))
            def _():
                pltpu.make_async_copy(far_ref.at[at, 0], ks.at[filled], sem.at[filled, 0]).start()
                pltpu.make_async_copy(far_ref.at[at, 1], vs.at[filled], sem.at[filled, 1]).start()

            return filled + inside.astype(jnp.int32)

        filled = lax.fori_loop(0, depth, begin, 0)
        fill[0] = filled

        def end(at, _):
            pltpu.make_async_copy(near_ref.at[0, 0], ks.at[at], sem.at[at, 0]).wait()
            pltpu.make_async_copy(near_ref.at[0, 1], vs.at[at], sem.at[at, 1]).wait()
            return 0

        lax.fori_loop(0, filled, end, 0)

    for target, source in ((m_ref, m_in), (l_ref, l_in), (a_ref, a_in)):
        target[0] = source[0]
    filled = fill[0]
    tiles = STRETCH // TILE

    def block(first, pages):
        rows = pages * PAGE
        keys = ks[pl.ds(first, pages)].reshape(rows, HD)
        values = vs[pl.ds(first, pages)].reshape(rows, HD)
        ahead = score(q_ref[:TILE, :], keys)
        for tile in range(tiles):
            scores = ahead
            if tile + 1 < tiles:
                ahead = score(q_ref[(tile + 1) * TILE : (tile + 2) * TILE, :], keys)
            here = slice(tile * TILE, (tile + 1) * TILE)
            m, l, a = online(scores, values, m_ref[0, here, :], l_ref[0, here, :], a_ref[0, here, :])
            m_ref[0, here, :] = m
            l_ref[0, here, :] = l
            a_ref[0, here, :] = a

    def fours(at, _):
        block(at * 4, 4)
        return 0

    lax.fori_loop(0, filled // 4, fours, 0)

    @pl.when(filled % 4 >= 2)
    def _():
        block(filled // 4 * 4, 2)

    @pl.when(filled % 2 == 1)
    def _():
        block(filled - 1, 1)

    if final:
        for tile in range(tiles):
            here = slice(tile * TILE, (tile + 1) * TILE)
            totals = jnp.sum(l_ref[0, here, :], axis=1, keepdims=True)
            o_ref[here, :] = (a_ref[0, here, :] / totals).astype(o_ref.dtype)


def shards(queries, stretch_keys, stretch_values, pool_keys, pool_values, page_counts, page_table):
    own_index = lax.axis_index("pool")
    heads = queries.shape[1] // HD
    chips = lax.axis_size("pool") // CORES
    own = own_index.astype(jnp.int32).reshape(1)
    depth = page_table.shape[2]
    table = page_table.reshape(-1, depth)
    far_first = list(range(chips))[::-1]
    picked = dict(zip(far_first, pick(own, table, pool_keys, pool_values, far_first)))

    other_keys = swapped(stretch_keys, "pool", 1)
    other_values = swapped(stretch_values, "pool", 1)
    params = pltpu.CompilerParams(vmem_limit_bytes=VMEM_BYTES)
    q_spec = pl.BlockSpec((STRETCH, HD), lambda h: (0, h))
    s_spec = pl.BlockSpec((1, STRETCH, HD), lambda h: (h, 0, 0))
    s_shape = jax.ShapeDtypeStruct((heads, STRETCH, HD), jnp.float32)
    state = pl.pallas_call(
        stretch_kernel,
        grid=(heads,),
        out_shape=[s_shape] * 3,
        in_specs=[SMEM, q_spec, ANY, ANY, ANY, ANY],
        out_specs=[s_spec] * 3,
        scratch_shapes=[
            pltpu.VMEM((STRETCH, HD), jnp.bfloat16),
            pltpu.VMEM((STRETCH, HD), jnp.bfloat16),
            pltpu.SemaphoreType.DMA((4,)),
        ],
        compiler_params=params,
        cost_estimate=pl.CostEstimate(flops=4 * 10**9, bytes_accessed=8 * 10**6, transcendentals=0),
        name="stretch",
    )(own, queries, stretch_keys, other_keys, stretch_values, other_values)

    cut = chips * 3 // 4
    for low, high in ((0, cut), (cut, chips)):
        final = high == chips
        got = [picked[at] if at == 0 else swapped(picked[at], "pool", at * CORES) for at in range(low, high)]
        mine = jnp.stack(got)
        others = swapped(mine, "pool", 1)
        most = min(depth, CORES * (high - low))
        scratch = [
            pltpu.VMEM((most, PAGE, HD), jnp.bfloat16),
            pltpu.VMEM((most, PAGE, HD), jnp.bfloat16),
            pltpu.SMEM((1,), jnp.int32),
        ]
        if final:
            scratch += [pltpu.VMEM((1, STRETCH, HD), jnp.float32)] * 3
        scratch.append(pltpu.SemaphoreType.DMA((most, 2)))
        state = pl.pallas_call(
            functools.partial(pages_kernel, low, high, final),
            grid=(heads,),
            out_shape=jax.ShapeDtypeStruct(queries.shape, queries.dtype) if final else [s_shape] * 3,
            in_specs=[SMEM, SMEM, SMEM, q_spec, ANY, ANY, s_spec, s_spec, s_spec],
            out_specs=q_spec if final else [s_spec] * 3,
            scratch_shapes=scratch,
            compiler_params=params,
            cost_estimate=pl.CostEstimate(flops=4 * 10**9, bytes_accessed=8 * 10**6, transcendentals=0),
            name="pages",
        )(own, table, page_counts, queries, mine, others, *state)
    return state


def solution(mesh):
    placed = (
        P(None, ("groups", "pool")),
        P(("groups", "pool"), None),
        P(("groups", "pool"), None),
        P(("groups", "pool"), None, None),
        P(("groups", "pool"), None, None),
        P("groups"),
        P("groups", None, None),
    )
    return jax.shard_map(
        shards, mesh=mesh, in_specs=placed, out_specs=P(None, ("groups", "pool")), check_vma=False
    )
```

```python
import functools
import math

import jax
import jax.numpy as jnp
from jax import lax
from jax.experimental import pallas as pl
from jax.experimental.pallas import tpu as pltpu
from jax.sharding import PartitionSpec as P

HD = 128
QH = 32
KVH = 4
PAGE = 256
STRETCH = 1024
SLOTS_DEV = 3
CORES = 2
TILE = 256
VMEM_BYTES = 24 * 2**20
EXP2_SCALE = math.log2(math.e) / math.sqrt(HD)
ROW_BY_ROW = (((1,), (1,)), ((), ()))

VMEM = pl.BlockSpec(memory_space=pltpu.VMEM)
SMEM = pl.BlockSpec(memory_space=pltpu.SMEM)
HBM = pl.BlockSpec(memory_space=pltpu.HBM)
ANY = pl.BlockSpec(memory_space=pl.ANY)
DONE = jax.ShapeDtypeStruct((8, HD), jnp.float32)


def swapped(value, axis, mask):
    pairs = [(source, source ^ mask) for source in range(lax.axis_size(axis))]
    return lax.ppermute(value, axis, pairs)


def pick_kernel(offsets, own_ref, table_ref, keys_ref, values_ref, *refs):
    outs, held, sem = refs[-2 - len(offsets) : -2], refs[-2], refs[-1]
    copies = [
        pltpu.make_async_copy(source, held.at[side], sem.at[side])
        for side, source in enumerate((keys_ref, values_ref))
    ]
    for copy in copies:
        copy.start()
    own = own_ref[0]
    first = own * SLOTS_DEV
    depth = table_ref.shape[1]
    slots = []
    for offset in offsets:
        row = jnp.bitwise_xor(own // CORES, offset)

        def look(page, slot, row=row):
            there = table_ref[row, page] - first
            return jnp.where((there >= 0) & (there < SLOTS_DEV), there, slot)

        slots.append(lax.fori_loop(0, depth, look, 0, unroll=True))
    for side, copy in enumerate(copies):
        copy.wait()
        for out, slot in zip(outs, slots):
            out[side] = held[side, slot]


def pick(own, table, keys, values, offsets, after=()):
    return pl.pallas_call(
        functools.partial(pick_kernel, offsets),
        out_shape=[jax.ShapeDtypeStruct((2, PAGE, HD), keys.dtype)] * len(offsets),
        in_specs=[SMEM, SMEM, HBM, HBM] + [ANY] * len(after),
        out_specs=[VMEM] * len(offsets),
        scratch_shapes=[pltpu.VMEM((2,) + keys.shape, keys.dtype), pltpu.SemaphoreType.DMA((2,))],
        compiler_params=pltpu.CompilerParams(vmem_limit_bytes=VMEM_BYTES),
        name="pick",
    )(own, table, keys, values, *after)


def pack_kernel(count, *refs):
    for at in range(count):
        refs[-1][at] = refs[at][...]


def pack(arrays, after):
    count = len(arrays)
    return pl.pallas_call(
        functools.partial(pack_kernel, count),
        out_shape=jax.ShapeDtypeStruct((count,) + arrays[0].shape, arrays[0].dtype),
        in_specs=[VMEM] * count + [ANY] * len(after),
        out_specs=VMEM,
        compiler_params=pltpu.CompilerParams(vmem_limit_bytes=VMEM_BYTES),
        name="pack",
    )(*arrays, *after)


def online(scores, values, old_max, old_totals, old_acc):
    width = scores.shape[1] // HD
    peak = jnp.max(scores, axis=1, keepdims=True)
    new_max = jnp.broadcast_to(peak, (scores.shape[0], HD))
    if old_max is not None:
        new_max = jnp.maximum(old_max, new_max)
    weights = jnp.exp2((scores - jnp.concatenate([new_max] * width, 1)) * EXP2_SCALE)
    totals = weights[:, :HD]
    for part in range(1, width):
        totals = totals + weights[:, part * HD : (part + 1) * HD]
    acc = jnp.dot(weights.astype(jnp.bfloat16), values, preferred_element_type=jnp.float32)
    if old_max is not None:
        rescale = jnp.exp2((old_max - new_max) * EXP2_SCALE)
        totals = old_totals * rescale + totals
        acc = old_acc * rescale + acc
    return new_max, totals, acc


def score(query, keys):
    return lax.dot_general(query, keys, ROW_BY_ROW, preferred_element_type=jnp.float32)


def stretch_kernel(own_ref, q_ref, k_ref, k2_ref, v_ref, v2_ref, m_ref, l_ref, a_ref, done_ref, ks, vs):
    half = own_ref[0] % CORES
    rows = k_ref.shape[0]
    for at, (source, target) in enumerate(((k_ref, ks), (k2_ref, ks), (v_ref, vs), (v2_ref, vs))):
        place = half if at % 2 == 0 else 1 - half
        target[pl.ds(pl.multiple_of(place * rows, rows), rows)] = source[...]
    done_ref[...] = jnp.zeros_like(done_ref)

    tiles = STRETCH // TILE
    row = lax.broadcasted_iota(jnp.int32, (TILE, TILE), 0)
    column = lax.broadcasted_iota(jnp.int32, (TILE, TILE), 1)

    def scores_of(h, tile):
        here = slice(tile * TILE, (tile + 1) * TILE)
        scores = score(q_ref[here, h * HD : (h + 1) * HD], ks[: (tile + 1) * TILE])
        last = jnp.where(column <= row, scores[:, tile * TILE :], -jnp.inf)
        if tile == 0:
            return last
        return jnp.concatenate([scores[:, : tile * TILE], last], 1)

    units = [(h, tile) for h in range(q_ref.shape[1] // HD) for tile in range(tiles)[::-1]]
    ahead = scores_of(*units[0])
    for at, (h, tile) in enumerate(units):
        scores = ahead
        if at + 1 < len(units):
            ahead = scores_of(*units[at + 1])
        here = slice(tile * TILE, (tile + 1) * TILE)
        m, l, a = online(scores, vs[: (tile + 1) * TILE], None, None, None)
        m_ref[h, here, :] = m
        l_ref[h, here, :] = l
        a_ref[h, here, :] = a


def pages_kernel(low, high, final, own_ref, table_ref, q_ref, near_ref, far_ref, m_in, l_in, a_in, *refs):
    if final:
        o_ref, ks, vs = refs
        m_ref, l_ref, a_ref = m_in, l_in, a_in
    else:
        m_ref, l_ref, a_ref, done_ref, ks, vs = refs
        done_ref[...] = jnp.zeros_like(done_ref)
    own = own_ref[0]
    chip = own // CORES
    core = own % CORES

    def begin(page, filled):
        slot = table_ref[chip, page]
        device = jnp.maximum(slot, 0) // SLOTS_DEV
        offset = jnp.bitwise_xor(device // CORES, chip)
        inside = (slot >= 0) & (offset >= low) & (offset < high)
        at = jnp.clip(offset - low, 0, high - low - 1)
        mine = device % CORES == core

        for source, there in ((near_ref, mine), (far_ref, jnp.logical_not(mine))):

            @pl.when(inside & there)
            def _():
                ks[filled] = source[at, 0]
                vs[filled] = source[at, 1]

        return filled + inside.astype(jnp.int32)

    filled = lax.fori_loop(0, table_ref.shape[1], begin, 0)
    tiles = STRETCH // TILE
    units = [(h, tile) for h in range(q_ref.shape[1] // HD) for tile in range(tiles)]

    def block(first, pages):
        rows = pages * PAGE
        keys = ks[pl.ds(first, pages)].reshape(rows, HD)
        values = vs[pl.ds(first, pages)].reshape(rows, HD)

        def scores_of(h, tile):
            return score(q_ref[tile * TILE : (tile + 1) * TILE, h * HD : (h + 1) * HD], keys)

        ahead = scores_of(*units[0])
        for at, (h, tile) in enumerate(units):
            scores = ahead
            if at + 1 < len(units):
                ahead = scores_of(*units[at + 1])
            here = slice(tile * TILE, (tile + 1) * TILE)
            m, l, a = online(scores, values, m_ref[h, here, :], l_ref[h, here, :], a_ref[h, here, :])
            m_ref[h, here, :] = m
            l_ref[h, here, :] = l
            a_ref[h, here, :] = a

    def fours(at, _):
        block(at * 4, 4)
        return 0

    lax.fori_loop(0, filled // 4, fours, 0)
    for pages in range(1, min(4, ks.shape[0] + 1)):

        @pl.when(filled % 4 == pages)
        def _():
            block(filled // 4 * 4, pages)

    if final:
        for h, tile in units:
            here = slice(tile * TILE, (tile + 1) * TILE)
            totals = jnp.sum(l_ref[h, here, :], axis=1, keepdims=True)
            o_ref[here, h * HD : (h + 1) * HD] = (a_ref[h, here, :] / totals).astype(o_ref.dtype)


def cost(flops):
    return pl.CostEstimate(flops=flops, bytes_accessed=8 * 10**6, transcendentals=0)


def attend_pages(low, high, final, own, table, queries, mine, others, state):
    depth = table.shape[1]
    most = min(depth, CORES * (high - low))
    s_shape = jax.ShapeDtypeStruct(state[0].shape, jnp.float32)
    return pl.pallas_call(
        functools.partial(pages_kernel, low, high, final),
        out_shape=jax.ShapeDtypeStruct(queries.shape, queries.dtype) if final else [s_shape] * 3 + [DONE],
        in_specs=[SMEM, SMEM, VMEM, VMEM, VMEM] + [VMEM] * 3,
        out_specs=VMEM if final else [VMEM] * 4,
        input_output_aliases={} if final else {5: 0, 6: 1, 7: 2},
        scratch_shapes=[
            pltpu.VMEM((most, PAGE, HD), jnp.bfloat16),
            pltpu.VMEM((most, PAGE, HD), jnp.bfloat16),
        ],
        compiler_params=pltpu.CompilerParams(vmem_limit_bytes=VMEM_BYTES),
        cost_estimate=cost(5 * 10**9),
        name="pages",
    )(own, table, queries, mine, others, *state[:3])


def shards(queries, stretch_keys, stretch_values, pool_keys, pool_values, page_counts, page_table):
    own_index = lax.axis_index("pool")
    heads = queries.shape[1] // HD
    chips = lax.axis_size("pool") // CORES
    own = own_index.astype(jnp.int32).reshape(1)
    depth = page_table.shape[2]
    table = page_table.reshape(-1, depth)
    near = list(range(chips // 2))
    far = list(range(chips // 2, chips * 3 // 4))
    last = list(range(chips * 3 // 4, chips))

    def sent(offset, value):
        return value if offset == 0 else swapped(value, "pool", offset * CORES)

    first = far + near[1:] + near[:1]
    picked = dict(zip(first, pick(own, table, pool_keys, pool_values, first)))
    got = {offset: sent(offset, picked[offset]) for offset in first}

    other_keys = swapped(stretch_keys, "pool", 1)
    other_values = swapped(stretch_values, "pool", 1)
    s_shape = jax.ShapeDtypeStruct((heads, STRETCH, HD), jnp.float32)
    state = pl.pallas_call(
        stretch_kernel,
        out_shape=[s_shape] * 3 + [DONE],
        in_specs=[SMEM] + [VMEM] * 5,
        out_specs=[VMEM] * 4,
        scratch_shapes=[
            pltpu.VMEM((STRETCH, HD), jnp.bfloat16),
            pltpu.VMEM((STRETCH, HD), jnp.bfloat16),
        ],
        compiler_params=pltpu.CompilerParams(vmem_limit_bytes=VMEM_BYTES),
        cost_estimate=cost(5 * 10**9),
        name="stretch",
    )(own, queries, stretch_keys, other_keys, stretch_values, other_values)

    rest = pick(own, table, pool_keys, pool_values, last, after=state[3:])
    for offset, value in zip(last, rest):
        got[offset] = sent(offset, value)

    for group in (far, near, last):
        mine = pack([got[offset] for offset in group], state[3:])
        others = swapped(mine, "pool", 1)
        low, high = group[0], group[-1] + 1
        state = attend_pages(low, high, group is last, own, table, queries, mine, others, state)
    return state


def solution(mesh):
    placed = (
        P(None, ("groups", "pool")),
        P(("groups", "pool"), None),
        P(("groups", "pool"), None),
        P(("groups", "pool"), None, None),
        P(("groups", "pool"), None, None),
        P("groups"),
        P("groups", None, None),
    )
    return jax.shard_map(
        shards, mesh=mesh, in_specs=placed, out_specs=P(None, ("groups", "pool")), check_vma=False
    )
```

```python
import functools
import math

import jax
import jax.numpy as jnp
from jax import lax
from jax.experimental import pallas as pl
from jax.experimental.pallas import tpu as pltpu
from jax.sharding import PartitionSpec as P

HD = 128
QH = 32
KVH = 4
PAGE = 256
STRETCH = 1024
SLOTS_DEV = 3
CORES = 2
TILE = 256
VMEM_BYTES = 24 * 2**20
PICK_VMEM = 56 * 2**20
BLOCK = 4
EXP2_SCALE = math.log2(math.e) / math.sqrt(HD)
ROW_BY_ROW = (((1,), (1,)), ((), ()))

VMEM = pl.BlockSpec(memory_space=pltpu.VMEM)
SMEM = pl.BlockSpec(memory_space=pltpu.SMEM)
ANY = pl.BlockSpec(memory_space=pl.ANY)
DONE = jax.ShapeDtypeStruct((8, HD), jnp.float32)


def swapped(value, axis, mask):
    pairs = [(source, source ^ mask) for source in range(lax.axis_size(axis))]
    return lax.ppermute(value, axis, pairs)


def pick_kernel(offsets, own_ref, table_ref, keys_ref, values_ref, *refs):
    outs, held, sem, sent = refs[:-3], refs[-3], refs[-2], refs[-1]
    loads = [
        pltpu.make_async_copy(source, held.at[side], sem.at[side])
        for side, source in enumerate((keys_ref, values_ref))
    ]
    for copy in loads:
        copy.start()
    own = own_ref[0]
    first = own * SLOTS_DEV
    key_heads, depth = table_ref.shape[1:]
    slots = []
    for offset in offsets:
        row = jnp.bitwise_xor(own // CORES, offset)

        def look(page, slot, row=row):
            there = table_ref[row // key_heads, row % key_heads, page] - first
            return jnp.where((there >= 0) & (there < SLOTS_DEV), there, slot)

        slots.append(lax.fori_loop(0, depth, look, 0, unroll=True))
    for copy in loads:
        copy.wait()
    stores = [
        pltpu.make_async_copy(held.at[side, slot], out.at[side], sent.at[at, side])
        for at, (out, slot) in enumerate(zip(outs, slots))
        for side in range(2)
    ]
    for copy in stores:
        copy.start()
    for copy in stores:
        copy.wait()


def pick(own, table, keys, values, offsets):
    return pl.pallas_call(
        functools.partial(pick_kernel, offsets),
        out_shape=[jax.ShapeDtypeStruct((2, PAGE, HD), keys.dtype)] * len(offsets),
        in_specs=[SMEM, SMEM, ANY, ANY],
        out_specs=[ANY] * len(offsets),
        scratch_shapes=[
            pltpu.VMEM((2,) + keys.shape, keys.dtype),
            pltpu.SemaphoreType.DMA((2,)),
            pltpu.SemaphoreType.DMA((len(offsets), 2)),
        ],
        compiler_params=pltpu.CompilerParams(vmem_limit_bytes=PICK_VMEM),
        name="pick",
    )(own, table, keys, values)


def pack_kernel(count, *refs):
    for at in range(count):
        refs[-1][at] = refs[at][...]


def pack(arrays, after):
    count = len(arrays)
    return pl.pallas_call(
        functools.partial(pack_kernel, count),
        out_shape=jax.ShapeDtypeStruct((count,) + arrays[0].shape, arrays[0].dtype),
        in_specs=[VMEM] * count + [ANY] * len(after),
        out_specs=VMEM,
        compiler_params=pltpu.CompilerParams(vmem_limit_bytes=VMEM_BYTES),
        name="pack",
    )(*arrays, *after)


def online(scores, values, old_max, old_totals, old_acc):
    width = scores.shape[1] // HD
    peak = jnp.max(scores, axis=1, keepdims=True)
    new_max = jnp.broadcast_to(peak, (scores.shape[0], HD))
    if old_max is not None:
        new_max = jnp.maximum(old_max, new_max)
    weights = jnp.exp2((scores - jnp.concatenate([new_max] * width, 1)) * EXP2_SCALE)
    totals = weights[:, :HD]
    for part in range(1, width):
        totals = totals + weights[:, part * HD : (part + 1) * HD]
    acc = jnp.dot(weights.astype(jnp.bfloat16), values, preferred_element_type=jnp.float32)
    if old_max is not None:
        rescale = jnp.exp2((old_max - new_max) * EXP2_SCALE)
        totals = old_totals * rescale + totals
        acc = old_acc * rescale + acc
    return new_max, totals, acc


def score(query, keys):
    return lax.dot_general(query, keys, ROW_BY_ROW, preferred_element_type=jnp.float32)


def list_pages(cuts, own, table_ref, list_ref):
    chip, core = own // CORES, own % CORES
    key_heads, depth = table_ref.shape[1:]
    seen = 0
    for wave in range(2):

        def look(page, seen, wave=wave):
            slot = table_ref[chip // key_heads, chip % key_heads, page]
            device = jnp.maximum(slot, 0) // SLOTS_DEV
            offset = jnp.bitwise_xor(device // CORES, chip)
            inside = (slot >= 0) & (offset >= cuts[wave]) & (offset < cuts[wave + 1])

            @pl.when(inside)
            def _():
                list_ref[2 + seen] = (offset - cuts[wave]) * 2 + jnp.bitwise_xor(device % CORES, core)

            return seen + inside.astype(jnp.int32)

        seen = lax.fori_loop(0, depth, look, seen)
        list_ref[wave] = seen


def stretch_kernel(cuts, own_ref, table_ref, q_ref, own_kv_ref, other_kv_ref, m_ref, l_ref, a_ref, done_ref, list_ref, ks, vs):
    list_pages(cuts, own_ref[0], table_ref, list_ref)
    half = own_ref[0] % CORES
    rows = own_kv_ref.shape[1]
    for place, source in ((half, own_kv_ref), (1 - half, other_kv_ref)):
        for side, target in enumerate((ks, vs)):
            target[pl.ds(pl.multiple_of(place * rows, rows), rows)] = source[side]
    done_ref[...] = jnp.zeros_like(done_ref)

    tiles = STRETCH // TILE
    row = lax.broadcasted_iota(jnp.int32, (TILE, TILE), 0)
    column = lax.broadcasted_iota(jnp.int32, (TILE, TILE), 1)

    def head(h, _):
        columns = pl.ds(pl.multiple_of(h * HD, HD), HD)

        def scores_of(tile):
            here = slice(tile * TILE, (tile + 1) * TILE)
            scores = score(q_ref[here, columns], ks[: (tile + 1) * TILE])
            last = jnp.where(column <= row, scores[:, tile * TILE :], -jnp.inf)
            if tile == 0:
                return last
            return jnp.concatenate([scores[:, : tile * TILE], last], 1)

        ahead = scores_of(tiles - 1)
        for tile in range(tiles)[::-1]:
            scores = ahead
            if tile > 0:
                ahead = scores_of(tile - 1)
            here = slice(tile * TILE, (tile + 1) * TILE)
            m, l, a = online(scores, vs[: (tile + 1) * TILE], None, None, None)
            m_ref[h, here, :] = m
            l_ref[h, here, :] = l
            a_ref[h, here, :] = a
        return 0

    lax.fori_loop(0, q_ref.shape[1] // HD, head, 0)


def pages_kernel(final, list_ref, q_ref, *refs):
    waves = 2 if final else 1
    sources = [(refs[2 * wave], refs[2 * wave + 1]) for wave in range(waves)]
    refs = refs[2 * waves :]
    if final:
        m_ref, l_ref, a_ref, o_ref, ks, vs, ahead_ref, held, sem = refs
    else:
        m_ref, l_ref, a_ref, done_ref, ks, vs, ahead_ref = refs[3:]
        done_ref[...] = jnp.zeros_like(done_ref)
    early = list_ref[0]
    skipped = early // BLOCK * BLOCK if final else 0
    spans = ((skipped, early), (early, list_ref[1])) if final else ((0, early // BLOCK * BLOCK),)
    for (start, stop), (near_ref, far_ref) in zip(spans, sources):

        def take(at, _, near_ref=near_ref, far_ref=far_ref):
            place = list_ref[2 + at]
            there = place // 2

            @pl.when(place % 2 == 0)
            def _():
                ks[at - skipped] = near_ref[there, 0]
                vs[at - skipped] = near_ref[there, 1]

            @pl.when(place % 2 == 1)
            def _():
                ks[at - skipped] = far_ref[there, 0]
                vs[at - skipped] = far_ref[there, 1]

            return 0

        lax.fori_loop(start, stop, take, 0)

    filled = list_ref[1] - skipped if final else early
    blocks = filled // BLOCK
    if final:
        blocks = (filled + BLOCK - 1) // BLOCK

        def blank(at, _):
            ks[at] = jnp.zeros((PAGE, HD), ks.dtype)
            vs[at] = jnp.zeros((PAGE, HD), vs.dtype)
            return 0

        lax.fori_loop(filled, blocks * BLOCK, blank, 0)
    heads = q_ref.shape[1] // HD
    tiles = STRETCH // TILE
    rows = BLOCK * PAGE
    units = [(h, tile) for h in range(heads) for tile in range(tiles)]

    def scores_of(first, h, tile):
        keys = ks[pl.ds(first, BLOCK)].reshape(rows, HD)
        queries = q_ref[tile * TILE : (tile + 1) * TILE, h * HD : (h + 1) * HD]
        scores = score(queries, keys)
        if final:
            key_at = lax.broadcasted_iota(jnp.int32, (1, rows), 1)
            scores = scores + jnp.where(key_at < (filled - first) * PAGE, 0.0, -jnp.inf)
        return scores

    @pl.when(blocks > 0)
    def _():
        ahead_ref[...] = scores_of(0, 0, 0)

    def block(at, _):
        first = at * BLOCK
        ahead = ahead_ref[...]
        for unit, (h, tile) in enumerate(units):
            scores = ahead
            if unit + 1 < len(units):
                ahead = scores_of(first, *units[unit + 1])
            else:
                ahead_ref[...] = scores_of(jnp.minimum(at + 1, blocks - 1) * BLOCK, 0, 0)
            values = vs[pl.ds(first, BLOCK)].reshape(rows, HD)
            here = slice(tile * TILE, (tile + 1) * TILE)
            m, l, a = online(scores, values, m_ref[h, here, :], l_ref[h, here, :], a_ref[h, here, :])
            m_ref[h, here, :] = m
            l_ref[h, here, :] = l
            a_ref[h, here, :] = a
        return 0

    lax.fori_loop(0, blocks, block, 0)

    if final:

        def out(h):
            columns = pl.ds(pl.multiple_of(h * HD, HD), HD)
            return pltpu.make_async_copy(held.at[h], o_ref.at[:, columns], sem.at[h])

        def finish(h, _):
            high = l_ref[h].astype(jnp.bfloat16)
            low = (l_ref[h] - high.astype(jnp.float32)).astype(jnp.bfloat16)
            ones = jnp.ones((2 * HD, HD), jnp.bfloat16)
            totals = jnp.dot(jnp.concatenate([high, low], 1), ones, preferred_element_type=jnp.float32)
            held[h] = (a_ref[h] / totals).astype(o_ref.dtype)
            out(h).start()
            return 0

        def leave(h, _):
            out(h).wait()
            return 0

        lax.fori_loop(0, heads, finish, 0)
        lax.fori_loop(0, heads, leave, 0)


COST = pl.CostEstimate(flops=1000, bytes_accessed=1000, transcendentals=0)


def attend_pages(cuts, final, pages, queries, received, state):
    waves = 2 if final else 1
    most = min(pages.shape[0] - 2, CORES * (cuts[1] - cuts[0]))
    if final:
        most = min(pages.shape[0] - 2, BLOCK - 1 + CORES * (cuts[2] - cuts[1]))
    most = -(-most // BLOCK) * BLOCK
    s_shape = jax.ShapeDtypeStruct(state[0].shape, jnp.float32)
    at = 2 + 2 * waves
    heads = state[0].shape[0]
    return pl.pallas_call(
        functools.partial(pages_kernel, final),
        out_shape=jax.ShapeDtypeStruct(queries.shape, queries.dtype) if final else [s_shape] * 3 + [DONE],
        in_specs=[SMEM] + [VMEM] * (4 + 2 * waves),
        out_specs=ANY if final else [VMEM] * 4,
        input_output_aliases={} if final else {at: 0, at + 1: 1, at + 2: 2},
        scratch_shapes=[
            pltpu.VMEM((most, PAGE, HD), jnp.bfloat16),
            pltpu.VMEM((most, PAGE, HD), jnp.bfloat16),
            pltpu.VMEM((TILE, BLOCK * PAGE), jnp.float32),
        ]
        + final * [pltpu.VMEM((heads, STRETCH, HD), queries.dtype), pltpu.SemaphoreType.DMA((heads,))],
        compiler_params=pltpu.CompilerParams(vmem_limit_bytes=VMEM_BYTES),
        cost_estimate=COST,
        name="pages",
    )(pages, queries, *received, *state[:3])


def shards(queries, stretch_keys, stretch_values, pool_keys, pool_values, page_counts, page_table):
    own_index = lax.axis_index("pool")
    heads = queries.shape[1] // HD
    chips = lax.axis_size("pool") // CORES
    own = own_index.astype(jnp.int32).reshape(1)
    cuts = (0, chips * 3 // 4, chips)
    order = list(range(chips // 2, chips)) + list(range(1, chips // 2)) + [0]
    picked = dict(zip(order, pick(own, page_table, pool_keys, pool_values, order)))
    got = {at: picked[at] if at == 0 else swapped(picked[at], "pool", at * CORES) for at in order}

    stretch = jnp.stack([stretch_keys, stretch_values])
    other_stretch = swapped(stretch, "pool", 1)
    s_shape = jax.ShapeDtypeStruct((heads, STRETCH, HD), jnp.float32)
    *state, pages = pl.pallas_call(
        functools.partial(stretch_kernel, cuts),
        out_shape=[s_shape] * 3 + [DONE, jax.ShapeDtypeStruct((2 + page_table.shape[2],), jnp.int32)],
        in_specs=[SMEM, SMEM] + [VMEM] * 3,
        out_specs=[VMEM] * 4 + [SMEM],
        scratch_shapes=[
            pltpu.VMEM((STRETCH, HD), jnp.bfloat16),
            pltpu.VMEM((STRETCH, HD), jnp.bfloat16),
        ],
        compiler_params=pltpu.CompilerParams(vmem_limit_bytes=VMEM_BYTES),
        cost_estimate=COST,
        name="stretch",
    )(own, page_table, queries, stretch, other_stretch)

    received = []
    for wave in range(2):
        mine = pack([got[at] for at in range(cuts[wave], cuts[wave + 1])], state[3:])
        received += [mine, swapped(mine, "pool", 1)]
        state = attend_pages(cuts, wave == 1, pages, queries, received, state)
    return state


def solution(mesh):
    placed = (
        P(None, ("groups", "pool")),
        P(("groups", "pool"), None),
        P(("groups", "pool"), None),
        P(("groups", "pool"), None, None),
        P(("groups", "pool"), None, None),
        P("groups"),
        P("groups", None, None),
    )
    return jax.shard_map(
        shards, mesh=mesh, in_specs=placed, out_specs=P(None, ("groups", "pool")), check_vma=False
    )
```

```python
import functools
import math

import jax
import jax.numpy as jnp
from jax import lax
from jax.experimental import pallas as pl
from jax.experimental.pallas import tpu as pltpu
from jax.sharding import PartitionSpec as P

HD = 128
QH = 32
KVH = 4
PAGE = 256
STRETCH = 1024
SLOTS_DEV = 3
CORES = 2
TILE = 256
VMEM_BYTES = 24 * 2**20
PICK_VMEM = 56 * 2**20
BLOCK = 4
WAVES = 2
HEAD = WAVES + 1
EXP2_SCALE = math.log2(math.e) / math.sqrt(HD)
ROW_BY_ROW = (((1,), (1,)), ((), ()))

VMEM = pl.BlockSpec(memory_space=pltpu.VMEM)
SMEM = pl.BlockSpec(memory_space=pltpu.SMEM)
ANY = pl.BlockSpec(memory_space=pl.ANY)
DONE = jax.ShapeDtypeStruct((8, HD), jnp.float32)


def swapped(value, axis, mask):
    pairs = [(source, source ^ mask) for source in range(lax.axis_size(axis))]
    return lax.ppermute(value, axis, pairs)


def pick_kernel(offsets, own_ref, table_ref, keys_ref, values_ref, *refs):
    outs, held, sem, sent = refs[:-3], refs[-3], refs[-2], refs[-1]
    loads = [
        pltpu.make_async_copy(source, held.at[side], sem.at[side])
        for side, source in enumerate((keys_ref, values_ref))
    ]
    for copy in loads:
        copy.start()
    own = own_ref[0]
    first = own * SLOTS_DEV
    key_heads, depth = table_ref.shape[1:]
    slots = []
    for offset in offsets:
        row = jnp.bitwise_xor(own // CORES, offset)

        def look(page, slot, row=row):
            there = table_ref[row // key_heads, row % key_heads, page] - first
            return jnp.where((there >= 0) & (there < SLOTS_DEV), there, slot)

        slots.append(lax.fori_loop(0, depth, look, 0, unroll=True))
    for copy in loads:
        copy.wait()
    stores = [
        pltpu.make_async_copy(held.at[side, slot], out.at[side], sent.at[at, side])
        for at, (out, slot) in enumerate(zip(outs, slots))
        for side in range(2)
    ]
    for copy in stores:
        copy.start()
    for copy in stores:
        copy.wait()


def pick(own, table, keys, values, offsets):
    return pl.pallas_call(
        functools.partial(pick_kernel, offsets),
        out_shape=[jax.ShapeDtypeStruct((2, PAGE, HD), keys.dtype)] * len(offsets),
        in_specs=[SMEM, SMEM, ANY, ANY],
        out_specs=[ANY] * len(offsets),
        scratch_shapes=[
            pltpu.VMEM((2,) + keys.shape, keys.dtype),
            pltpu.SemaphoreType.DMA((2,)),
            pltpu.SemaphoreType.DMA((len(offsets), 2)),
        ],
        compiler_params=pltpu.CompilerParams(vmem_limit_bytes=PICK_VMEM),
        name="pick",
    )(own, table, keys, values)


def pack_kernel(count, *refs):
    for at in range(count):
        refs[-1][at] = refs[at][...]


def pack(arrays, after):
    count = len(arrays)
    return pl.pallas_call(
        functools.partial(pack_kernel, count),
        out_shape=jax.ShapeDtypeStruct((count,) + arrays[0].shape, arrays[0].dtype),
        in_specs=[VMEM] * count + [ANY] * len(after),
        out_specs=VMEM,
        compiler_params=pltpu.CompilerParams(vmem_limit_bytes=VMEM_BYTES),
        name="pack",
    )(*arrays, *after)


def online(scores, values, old_max, old_totals, old_acc):
    width = scores.shape[1] // HD
    peak = jnp.max(scores, axis=1, keepdims=True)
    new_max = jnp.broadcast_to(peak, (scores.shape[0], HD))
    if old_max is not None:
        new_max = jnp.maximum(old_max, new_max)
    weights = jnp.exp2((scores - jnp.concatenate([new_max] * width, 1)) * EXP2_SCALE)
    totals = weights[:, :HD]
    for part in range(1, width):
        totals = totals + weights[:, part * HD : (part + 1) * HD]
    acc = jnp.dot(weights.astype(jnp.bfloat16), values, preferred_element_type=jnp.float32)
    if old_max is not None:
        rescale = jnp.exp2((old_max - new_max) * EXP2_SCALE)
        totals = old_totals * rescale + totals
        acc = old_acc * rescale + acc
    return new_max, totals, acc


def score(query, keys):
    return lax.dot_general(query, keys, ROW_BY_ROW, preferred_element_type=jnp.float32)


def list_pages(cuts, own, table_ref, list_ref):
    chip, core = own // CORES, own % CORES
    key_heads, depth = table_ref.shape[1:]
    seen = 0
    for wave in range(WAVES):

        def look(page, seen, wave=wave):
            slot = table_ref[chip // key_heads, chip % key_heads, page]
            device = jnp.maximum(slot, 0) // SLOTS_DEV
            offset = jnp.bitwise_xor(device // CORES, chip)
            inside = (slot >= 0) & (offset >= cuts[wave]) & (offset < cuts[wave + 1])

            @pl.when(inside)
            def _():
                list_ref[HEAD + seen] = (offset - cuts[wave]) * 2 + jnp.bitwise_xor(device % CORES, core)

            return seen + inside.astype(jnp.int32)

        seen = lax.fori_loop(0, depth, look, seen)
        list_ref[wave] = seen
    early = list_ref[WAVES - 2]
    late = seen - early
    rest = early % BLOCK
    more = (rest + late + BLOCK - 1) // BLOCK > (late + BLOCK - 1) // BLOCK
    list_ref[WAVES] = jnp.where(more, early, early - rest)


def stretch_kernel(cuts, own_ref, table_ref, q_ref, own_kv_ref, other_kv_ref, m_ref, l_ref, a_ref, done_ref, list_ref, ks, vs):
    list_pages(cuts, own_ref[0], table_ref, list_ref)
    half = own_ref[0] % CORES
    rows = own_kv_ref.shape[1]
    for place, source in ((half, own_kv_ref), (1 - half, other_kv_ref)):
        for side, target in enumerate((ks, vs)):
            target[pl.ds(pl.multiple_of(place * rows, rows), rows)] = source[side]
    done_ref[...] = jnp.zeros_like(done_ref)

    tiles = STRETCH // TILE
    row = lax.broadcasted_iota(jnp.int32, (TILE, TILE), 0)
    column = lax.broadcasted_iota(jnp.int32, (TILE, TILE), 1)

    def head(h, _):
        columns = pl.ds(pl.multiple_of(h * HD, HD), HD)

        def scores_of(tile):
            here = slice(tile * TILE, (tile + 1) * TILE)
            scores = score(q_ref[here, columns], ks[: (tile + 1) * TILE])
            last = jnp.where(column <= row, scores[:, tile * TILE :], -jnp.inf)
            if tile == 0:
                return last
            return jnp.concatenate([scores[:, : tile * TILE], last], 1)

        ahead = scores_of(tiles - 1)
        for tile in range(tiles)[::-1]:
            scores = ahead
            if tile > 0:
                ahead = scores_of(tile - 1)
            here = slice(tile * TILE, (tile + 1) * TILE)
            m, l, a = online(scores, vs[: (tile + 1) * TILE], None, None, None)
            m_ref[h, here, :] = m
            l_ref[h, here, :] = l
            a_ref[h, here, :] = a
        return 0

    lax.fori_loop(0, q_ref.shape[1] // HD, head, 0)


def pages_kernel(final, list_ref, q_ref, *refs):
    waves = WAVES if final else WAVES - 1
    sources = [(refs[2 * wave], refs[2 * wave + 1]) for wave in range(waves)]
    refs = refs[2 * waves :]
    if final:
        m_ref, l_ref, a_ref, o_ref, ks, vs, ahead_ref, held, sem = refs
    else:
        m_ref, l_ref, a_ref, done_ref, ks, vs, ahead_ref = refs[3:]
        done_ref[...] = jnp.zeros_like(done_ref)
    skipped = list_ref[WAVES] if final else 0
    limit = list_ref[WAVES - 1] if final else list_ref[WAVES]
    for wave, (near_ref, far_ref) in enumerate(sources):
        start = jnp.maximum(list_ref[wave - 1], skipped) if wave > 0 else skipped
        stop = jnp.minimum(list_ref[wave], limit)

        def take(at, _, near_ref=near_ref, far_ref=far_ref):
            place = list_ref[HEAD + at]
            there = place // 2

            @pl.when(place % 2 == 0)
            def _():
                ks[at - skipped] = near_ref[there, 0]
                vs[at - skipped] = near_ref[there, 1]

            @pl.when(place % 2 == 1)
            def _():
                ks[at - skipped] = far_ref[there, 0]
                vs[at - skipped] = far_ref[there, 1]

            return 0

        lax.fori_loop(start, stop, take, 0)

    filled = limit - skipped
    blocks = (filled + BLOCK - 1) // BLOCK

    def blank(at, _):
        ks[at] = jnp.zeros((PAGE, HD), ks.dtype)
        vs[at] = jnp.zeros((PAGE, HD), vs.dtype)
        return 0

    lax.fori_loop(filled, blocks * BLOCK, blank, 0)
    heads = q_ref.shape[1] // HD
    tiles = STRETCH // TILE
    rows = BLOCK * PAGE
    units = [(h, tile) for h in range(heads) for tile in range(tiles)]

    def scores_of(first, h, tile):
        keys = ks[pl.ds(first, BLOCK)].reshape(rows, HD)
        queries = q_ref[tile * TILE : (tile + 1) * TILE, h * HD : (h + 1) * HD]
        key_at = lax.broadcasted_iota(jnp.int32, (1, rows), 1)
        return score(queries, keys) + jnp.where(key_at < (filled - first) * PAGE, 0.0, -jnp.inf)

    @pl.when(blocks > 0)
    def _():
        ahead_ref[...] = scores_of(0, 0, 0)

    def block(at, _):
        first = at * BLOCK
        ahead = ahead_ref[...]
        for unit, (h, tile) in enumerate(units):
            scores = ahead
            if unit + 1 < len(units):
                ahead = scores_of(first, *units[unit + 1])
            else:
                ahead_ref[...] = scores_of(jnp.minimum(at + 1, blocks - 1) * BLOCK, 0, 0)
            values = vs[pl.ds(first, BLOCK)].reshape(rows, HD)
            here = slice(tile * TILE, (tile + 1) * TILE)
            m, l, a = online(scores, values, m_ref[h, here, :], l_ref[h, here, :], a_ref[h, here, :])
            m_ref[h, here, :] = m
            l_ref[h, here, :] = l
            a_ref[h, here, :] = a
        return 0

    lax.fori_loop(0, blocks, block, 0)

    if final:

        def out(h):
            columns = pl.ds(pl.multiple_of(h * HD, HD), HD)
            return pltpu.make_async_copy(held.at[h], o_ref.at[:, columns], sem.at[h])

        def finish(h, _):
            high = l_ref[h].astype(jnp.bfloat16)
            low = (l_ref[h] - high.astype(jnp.float32)).astype(jnp.bfloat16)
            ones = jnp.ones((2 * HD, HD), jnp.bfloat16)
            totals = jnp.dot(jnp.concatenate([high, low], 1), ones, preferred_element_type=jnp.float32)
            held[h] = (a_ref[h] / totals).astype(o_ref.dtype)
            out(h).start()
            return 0

        def leave(h, _):
            out(h).wait()
            return 0

        lax.fori_loop(0, heads, finish, 0)
        lax.fori_loop(0, heads, leave, 0)


COST = pl.CostEstimate(flops=1000, bytes_accessed=1000, transcendentals=0)


def attend_pages(cuts, final, pages, queries, received, state):
    waves = WAVES if final else WAVES - 1
    most = CORES * cuts[WAVES - 1]
    if final:
        most = BLOCK - 1 + CORES * (cuts[WAVES] - cuts[WAVES - 1])
    most = min(pages.shape[0] - HEAD, most)
    most = -(-most // BLOCK) * BLOCK
    s_shape = jax.ShapeDtypeStruct(state[0].shape, jnp.float32)
    at = 2 + 2 * waves
    heads = state[0].shape[0]
    return pl.pallas_call(
        functools.partial(pages_kernel, final),
        out_shape=jax.ShapeDtypeStruct(queries.shape, queries.dtype) if final else [s_shape] * 3 + [DONE],
        in_specs=[SMEM] + [VMEM] * (4 + 2 * waves),
        out_specs=ANY if final else [VMEM] * 4,
        input_output_aliases={} if final else {at: 0, at + 1: 1, at + 2: 2},
        scratch_shapes=[
            pltpu.VMEM((most, PAGE, HD), jnp.bfloat16),
            pltpu.VMEM((most, PAGE, HD), jnp.bfloat16),
            pltpu.VMEM((TILE, BLOCK * PAGE), jnp.float32),
        ]
        + final * [pltpu.VMEM((heads, STRETCH, HD), queries.dtype), pltpu.SemaphoreType.DMA((heads,))],
        compiler_params=pltpu.CompilerParams(vmem_limit_bytes=VMEM_BYTES),
        cost_estimate=COST,
        name="pages",
    )(pages, queries, *received, *state[:3])


def shards(queries, stretch_keys, stretch_values, pool_keys, pool_values, page_counts, page_table):
    own_index = lax.axis_index("pool")
    heads = queries.shape[1] // HD
    chips = lax.axis_size("pool") // CORES
    own = own_index.astype(jnp.int32).reshape(1)
    cuts = (0, chips * 3 // 4, chips)
    order = list(range(chips // 2, chips)) + list(range(1, chips // 2)) + [0]
    picked = dict(zip(order, pick(own, page_table, pool_keys, pool_values, order)))
    got = {at: picked[at] if at == 0 else swapped(picked[at], "pool", at * CORES) for at in order}

    stretch = jnp.stack([stretch_keys, stretch_values])
    other_stretch = swapped(stretch, "pool", 1)
    s_shape = jax.ShapeDtypeStruct((heads, STRETCH, HD), jnp.float32)
    *state, pages = pl.pallas_call(
        functools.partial(stretch_kernel, cuts),
        out_shape=[s_shape] * 3 + [DONE, jax.ShapeDtypeStruct((HEAD + page_table.shape[2],), jnp.int32)],
        in_specs=[SMEM, SMEM] + [VMEM] * 3,
        out_specs=[VMEM] * 4 + [SMEM],
        scratch_shapes=[
            pltpu.VMEM((STRETCH, HD), jnp.bfloat16),
            pltpu.VMEM((STRETCH, HD), jnp.bfloat16),
        ],
        compiler_params=pltpu.CompilerParams(vmem_limit_bytes=VMEM_BYTES),
        cost_estimate=COST,
        name="stretch",
    )(own, page_table, queries, stretch, other_stretch)

    received = []
    after = state[3:]
    for wave in range(WAVES):
        mine = pack([got[at] for at in range(cuts[wave], cuts[wave + 1])], after)
        received += [mine, swapped(mine, "pool", 1)]
        after = [mine]
        if wave >= WAVES - 2:
            state = attend_pages(cuts, wave == WAVES - 1, pages, queries, received, state)
            after = state[3:]
    return state


def solution(mesh):
    placed = (
        P(None, ("groups", "pool")),
        P(("groups", "pool"), None),
        P(("groups", "pool"), None),
        P(("groups", "pool"), None, None),
        P(("groups", "pool"), None, None),
        P("groups"),
        P("groups", None, None),
    )
    return jax.shard_map(
        shards, mesh=mesh, in_specs=placed, out_specs=P(None, ("groups", "pool")), check_vma=False
    )
```

```python
import functools
import math

import jax
import jax.numpy as jnp
from jax import lax
from jax.experimental import pallas as pl
from jax.experimental.pallas import tpu as pltpu
from jax.sharding import PartitionSpec as P

HD = 128
QH = 32
KVH = 4
PAGE = 256
STRETCH = 1024
SLOTS_DEV = 3
CORES = 2
TILE = 256
VMEM_BYTES = 24 * 2**20
PICK_VMEM = 56 * 2**20
BLOCK = 4
WAVES = 2
HEAD = WAVES + 1
EXP2_SCALE = math.log2(math.e) / math.sqrt(HD)
ROW_BY_ROW = (((1,), (1,)), ((), ()))

VMEM = pl.BlockSpec(memory_space=pltpu.VMEM)
SMEM = pl.BlockSpec(memory_space=pltpu.SMEM)
ANY = pl.BlockSpec(memory_space=pl.ANY)
DONE = jax.ShapeDtypeStruct((8, HD), jnp.float32)


def swapped(value, axis, mask):
    pairs = [(source, source ^ mask) for source in range(lax.axis_size(axis))]
    return lax.ppermute(value, axis, pairs)


def pick_kernel(offsets, own_ref, table_ref, keys_ref, values_ref, *refs):
    outs, held, sem, sent = refs[:-3], refs[-3], refs[-2], refs[-1]
    loads = [
        pltpu.make_async_copy(source, held.at[side], sem.at[side])
        for side, source in enumerate((keys_ref, values_ref))
    ]
    for copy in loads:
        copy.start()
    own = own_ref[0]
    first = own * SLOTS_DEV
    key_heads, depth = table_ref.shape[1:]
    slots = []
    for offset in offsets:
        row = jnp.bitwise_xor(own // CORES, offset)

        def look(page, slot, row=row):
            there = table_ref[row // key_heads, row % key_heads, page] - first
            return jnp.where((there >= 0) & (there < SLOTS_DEV), there, slot)

        slots.append(lax.fori_loop(0, depth, look, 0, unroll=True))
    for copy in loads:
        copy.wait()
    stores = [
        pltpu.make_async_copy(held.at[side, slot], out.at[side], sent.at[at, side])
        for at, (out, slot) in enumerate(zip(outs, slots))
        for side in range(2)
    ]
    for copy in stores:
        copy.start()
    for copy in stores:
        copy.wait()


def pick(own, table, keys, values, offsets):
    return pl.pallas_call(
        functools.partial(pick_kernel, offsets),
        out_shape=[jax.ShapeDtypeStruct((2, PAGE, HD), keys.dtype)] * len(offsets),
        in_specs=[SMEM, SMEM, ANY, ANY],
        out_specs=[ANY] * len(offsets),
        scratch_shapes=[
            pltpu.VMEM((2,) + keys.shape, keys.dtype),
            pltpu.SemaphoreType.DMA((2,)),
            pltpu.SemaphoreType.DMA((len(offsets), 2)),
        ],
        compiler_params=pltpu.CompilerParams(vmem_limit_bytes=PICK_VMEM),
        name="pick",
    )(own, table, keys, values)


def pack_kernel(count, *refs):
    for at in range(count):
        refs[-1][at] = refs[at][...]


def pack(arrays, after):
    count = len(arrays)
    return pl.pallas_call(
        functools.partial(pack_kernel, count),
        out_shape=jax.ShapeDtypeStruct((count,) + arrays[0].shape, arrays[0].dtype),
        in_specs=[VMEM] * count + [ANY] * len(after),
        out_specs=VMEM,
        compiler_params=pltpu.CompilerParams(vmem_limit_bytes=VMEM_BYTES),
        name="pack",
    )(*arrays, *after)


def online(scores, values, old_max, old_totals, old_acc):
    width = scores.shape[1] // HD
    peak = jnp.max(scores, axis=1, keepdims=True)
    new_max = jnp.broadcast_to(peak, (scores.shape[0], HD))
    if old_max is not None:
        new_max = jnp.maximum(old_max, new_max)
    weights = jnp.exp2((scores - jnp.concatenate([new_max] * width, 1)) * EXP2_SCALE)
    totals = weights[:, :HD]
    for part in range(1, width):
        totals = totals + weights[:, part * HD : (part + 1) * HD]
    acc = jnp.dot(weights.astype(jnp.bfloat16), values, preferred_element_type=jnp.float32)
    if old_max is not None:
        rescale = jnp.exp2((old_max - new_max) * EXP2_SCALE)
        totals = old_totals * rescale + totals
        acc = old_acc * rescale + acc
    return new_max, totals, acc


def score(query, keys):
    return lax.dot_general(query, keys, ROW_BY_ROW, preferred_element_type=jnp.float32)


def list_pages(cuts, own, table_ref, list_ref):
    chip, core = own // CORES, own % CORES
    key_heads, depth = table_ref.shape[1:]
    seen = 0
    for wave in range(WAVES):

        def look(page, seen, wave=wave):
            slot = table_ref[chip // key_heads, chip % key_heads, page]
            device = jnp.maximum(slot, 0) // SLOTS_DEV
            offset = jnp.bitwise_xor(device // CORES, chip)
            inside = (slot >= 0) & (offset >= cuts[wave]) & (offset < cuts[wave + 1])

            @pl.when(inside)
            def _():
                list_ref[HEAD + seen] = (cuts[wave + 1] - 1 - offset) * 2 + jnp.bitwise_xor(device % CORES, core)

            return seen + inside.astype(jnp.int32)

        seen = lax.fori_loop(0, depth, look, seen)
        list_ref[wave] = seen
    early = list_ref[WAVES - 2]
    late = seen - early
    rest = early % BLOCK
    more = (rest + late + BLOCK - 1) // BLOCK > (late + BLOCK - 1) // BLOCK
    list_ref[WAVES] = jnp.where(more, early, early - rest)


def stretch_kernel(cuts, own_ref, table_ref, q_ref, own_kv_ref, other_kv_ref, m_ref, l_ref, a_ref, done_ref, list_ref, ks, vs):
    list_pages(cuts, own_ref[0], table_ref, list_ref)
    half = own_ref[0] % CORES
    rows = own_kv_ref.shape[1]
    for place, source in ((half, own_kv_ref), (1 - half, other_kv_ref)):
        for side, target in enumerate((ks, vs)):
            target[pl.ds(pl.multiple_of(place * rows, rows), rows)] = source[side]
    done_ref[...] = jnp.zeros_like(done_ref)

    tiles = STRETCH // TILE
    row = lax.broadcasted_iota(jnp.int32, (TILE, TILE), 0)
    column = lax.broadcasted_iota(jnp.int32, (TILE, TILE), 1)

    def head(h, _):
        columns = pl.ds(pl.multiple_of(h * HD, HD), HD)

        def scores_of(tile):
            here = slice(tile * TILE, (tile + 1) * TILE)
            scores = score(q_ref[here, columns], ks[: (tile + 1) * TILE])
            last = jnp.where(column <= row, scores[:, tile * TILE :], -jnp.inf)
            if tile == 0:
                return last
            return jnp.concatenate([scores[:, : tile * TILE], last], 1)

        ahead = scores_of(tiles - 1)
        for tile in range(tiles)[::-1]:
            scores = ahead
            if tile > 0:
                ahead = scores_of(tile - 1)
            here = slice(tile * TILE, (tile + 1) * TILE)
            m, l, a = online(scores, vs[: (tile + 1) * TILE], None, None, None)
            m_ref[h, here, :] = m
            l_ref[h, here, :] = l
            a_ref[h, here, :] = a
        return 0

    lax.fori_loop(0, q_ref.shape[1] // HD, head, 0)


def pages_kernel(final, list_ref, q_ref, *refs):
    waves = WAVES if final else WAVES - 1
    sources = [(refs[2 * wave], refs[2 * wave + 1]) for wave in range(waves)]
    refs = refs[2 * waves :]
    if final:
        m_ref, l_ref, a_ref, o_ref, ks, vs, ahead_ref, held, sem = refs
    else:
        m_ref, l_ref, a_ref, done_ref, ks, vs, ahead_ref = refs[3:]
        done_ref[...] = jnp.zeros_like(done_ref)
    skipped = list_ref[WAVES] if final else 0
    limit = list_ref[WAVES - 1] if final else list_ref[WAVES]
    for wave, (near_ref, far_ref) in enumerate(sources):
        start = jnp.maximum(list_ref[wave - 1], skipped) if wave > 0 else skipped
        stop = jnp.minimum(list_ref[wave], limit)

        def take(at, _, near_ref=near_ref, far_ref=far_ref):
            place = list_ref[HEAD + at]
            there = place // 2

            @pl.when(place % 2 == 0)
            def _():
                ks[at - skipped] = near_ref[there, 0]
                vs[at - skipped] = near_ref[there, 1]

            @pl.when(place % 2 == 1)
            def _():
                ks[at - skipped] = far_ref[there, 0]
                vs[at - skipped] = far_ref[there, 1]

            return 0

        lax.fori_loop(start, stop, take, 0)

    filled = limit - skipped
    blocks = (filled + BLOCK - 1) // BLOCK

    def blank(at, _):
        ks[at] = jnp.zeros((PAGE, HD), ks.dtype)
        vs[at] = jnp.zeros((PAGE, HD), vs.dtype)
        return 0

    lax.fori_loop(filled, blocks * BLOCK, blank, 0)
    heads = q_ref.shape[1] // HD
    tiles = STRETCH // TILE
    rows = BLOCK * PAGE
    units = [(h, tile) for h in range(heads) for tile in range(tiles)]

    def scores_of(first, h, tile):
        keys = ks[pl.ds(first, BLOCK)].reshape(rows, HD)
        queries = q_ref[tile * TILE : (tile + 1) * TILE, h * HD : (h + 1) * HD]
        key_at = lax.broadcasted_iota(jnp.int32, (1, rows), 1)
        return score(queries, keys) + jnp.where(key_at < (filled - first) * PAGE, 0.0, -jnp.inf)

    @pl.when(blocks > 0)
    def _():
        ahead_ref[...] = scores_of(0, 0, 0)

    def block(at, _):
        first = at * BLOCK
        ahead = ahead_ref[...]
        for unit, (h, tile) in enumerate(units):
            scores = ahead
            if unit + 1 < len(units):
                ahead = scores_of(first, *units[unit + 1])
            else:
                ahead_ref[...] = scores_of(jnp.minimum(at + 1, blocks - 1) * BLOCK, 0, 0)
            values = vs[pl.ds(first, BLOCK)].reshape(rows, HD)
            here = slice(tile * TILE, (tile + 1) * TILE)
            m, l, a = online(scores, values, m_ref[h, here, :], l_ref[h, here, :], a_ref[h, here, :])
            m_ref[h, here, :] = m
            l_ref[h, here, :] = l
            a_ref[h, here, :] = a
        return 0

    lax.fori_loop(0, blocks, block, 0)

    if final:

        def out(h):
            columns = pl.ds(pl.multiple_of(h * HD, HD), HD)
            return pltpu.make_async_copy(held.at[h], o_ref.at[:, columns], sem.at[h])

        def finish(h, _):
            high = l_ref[h].astype(jnp.bfloat16)
            low = (l_ref[h] - high.astype(jnp.float32)).astype(jnp.bfloat16)
            ones = jnp.ones((2 * HD, HD), jnp.bfloat16)
            totals = jnp.dot(jnp.concatenate([high, low], 1), ones, preferred_element_type=jnp.float32)
            held[h] = (a_ref[h] / totals).astype(o_ref.dtype)
            out(h).start()
            return 0

        def leave(h, _):
            out(h).wait()
            return 0

        lax.fori_loop(0, heads, finish, 0)
        lax.fori_loop(0, heads, leave, 0)


COST = pl.CostEstimate(flops=1000, bytes_accessed=1000, transcendentals=0)


def attend_pages(cuts, final, pages, queries, received, state):
    waves = WAVES if final else WAVES - 1
    most = CORES * cuts[WAVES - 1]
    if final:
        most = BLOCK - 1 + CORES * (cuts[WAVES] - cuts[WAVES - 1])
    most = min(pages.shape[0] - HEAD, most)
    most = -(-most // BLOCK) * BLOCK
    s_shape = jax.ShapeDtypeStruct(state[0].shape, jnp.float32)
    at = 2 + 2 * waves
    heads = state[0].shape[0]
    return pl.pallas_call(
        functools.partial(pages_kernel, final),
        out_shape=jax.ShapeDtypeStruct(queries.shape, queries.dtype) if final else [s_shape] * 3 + [DONE],
        in_specs=[SMEM] + [VMEM] * (4 + 2 * waves),
        out_specs=ANY if final else [VMEM] * 4,
        input_output_aliases={} if final else {at: 0, at + 1: 1, at + 2: 2},
        scratch_shapes=[
            pltpu.VMEM((most, PAGE, HD), jnp.bfloat16),
            pltpu.VMEM((most, PAGE, HD), jnp.bfloat16),
            pltpu.VMEM((TILE, BLOCK * PAGE), jnp.float32),
        ]
        + final * [pltpu.VMEM((heads, STRETCH, HD), queries.dtype), pltpu.SemaphoreType.DMA((heads,))],
        compiler_params=pltpu.CompilerParams(vmem_limit_bytes=VMEM_BYTES),
        cost_estimate=COST,
        name="pages",
    )(pages, queries, *received, *state[:3])


def shards(queries, stretch_keys, stretch_values, pool_keys, pool_values, page_counts, page_table):
    own_index = lax.axis_index("pool")
    heads = queries.shape[1] // HD
    chips = lax.axis_size("pool") // CORES
    own = own_index.astype(jnp.int32).reshape(1)
    cuts = (0, chips * 3 // 4, chips)
    order = list(range(chips // 2, chips)) + list(range(1, chips // 2)) + [0]
    picked = dict(zip(order, pick(own, page_table, pool_keys, pool_values, order)))
    got = {at: picked[at] if at == 0 else swapped(picked[at], "pool", at * CORES) for at in order}

    stretch = jnp.stack([stretch_keys, stretch_values])
    other_stretch = swapped(stretch, "pool", 1)
    s_shape = jax.ShapeDtypeStruct((heads, STRETCH, HD), jnp.float32)
    *state, pages = pl.pallas_call(
        functools.partial(stretch_kernel, cuts),
        out_shape=[s_shape] * 3 + [DONE, jax.ShapeDtypeStruct((HEAD + page_table.shape[2],), jnp.int32)],
        in_specs=[SMEM, SMEM] + [VMEM] * 3,
        out_specs=[VMEM] * 4 + [SMEM],
        scratch_shapes=[
            pltpu.VMEM((STRETCH, HD), jnp.bfloat16),
            pltpu.VMEM((STRETCH, HD), jnp.bfloat16),
        ],
        compiler_params=pltpu.CompilerParams(vmem_limit_bytes=VMEM_BYTES),
        cost_estimate=COST,
        name="stretch",
    )(own, page_table, queries, stretch, other_stretch)

    received = []
    after = state[3:]
    for wave in range(WAVES):
        mine = pack([got[at] for at in range(cuts[wave], cuts[wave + 1])[::-1]], after)
        received += [mine, swapped(mine, "pool", 1)]
        after = [mine]
        if wave >= WAVES - 2:
            state = attend_pages(cuts, wave == WAVES - 1, pages, queries, received, state)
            after = state[3:]
    return state


def solution(mesh):
    placed = (
        P(None, ("groups", "pool")),
        P(("groups", "pool"), None),
        P(("groups", "pool"), None),
        P(("groups", "pool"), None, None),
        P(("groups", "pool"), None, None),
        P("groups"),
        P("groups", None, None),
    )
    return jax.shard_map(
        shards, mesh=mesh, in_specs=placed, out_specs=P(None, ("groups", "pool")), check_vma=False
    )
```

```python
import functools
import math

import jax
import jax.numpy as jnp
from jax import lax
from jax.experimental import pallas as pl
from jax.experimental.pallas import tpu as pltpu
from jax.sharding import PartitionSpec as P

HD = 128
QH = 32
KVH = 4
PAGE = 256
STRETCH = 1024
SLOTS_DEV = 3
CORES = 2
TILE = 256
VMEM_BYTES = 24 * 2**20
PICK_VMEM = 56 * 2**20
BLOCK = 4
WAVES = 2
HEAD = WAVES + 1
EXP2_SCALE = math.log2(math.e) / math.sqrt(HD)
ROW_BY_ROW = (((1,), (1,)), ((), ()))

VMEM = pl.BlockSpec(memory_space=pltpu.VMEM)
SMEM = pl.BlockSpec(memory_space=pltpu.SMEM)
ANY = pl.BlockSpec(memory_space=pl.ANY)
DONE = jax.ShapeDtypeStruct((8, HD), jnp.float32)


def swapped(value, axis, mask):
    pairs = [(source, source ^ mask) for source in range(lax.axis_size(axis))]
    return lax.ppermute(value, axis, pairs)


def pick_kernel(offsets, own_ref, table_ref, keys_ref, values_ref, new_keys_ref, new_values_ref, *refs):
    *outs, new_out, held, new_held, sem, sent = refs
    loads = [
        pltpu.make_async_copy(source, held.at[side], sem.at[side])
        for side, source in enumerate((keys_ref, values_ref))
    ]
    loads += [
        pltpu.make_async_copy(source, new_held.at[side], sem.at[2 + side])
        for side, source in enumerate((new_keys_ref, new_values_ref))
    ]
    for copy in loads:
        copy.start()
    own = own_ref[0]
    first = own * SLOTS_DEV
    key_heads, depth = table_ref.shape[1:]
    slots = []
    for offset in offsets:
        row = jnp.bitwise_xor(own // CORES, offset)

        def look(page, slot, row=row):
            there = table_ref[row // key_heads, row % key_heads, page] - first
            return jnp.where((there >= 0) & (there < SLOTS_DEV), there, slot)

        slots.append(lax.fori_loop(0, depth, look, 0, unroll=True))
    for copy in loads:
        copy.wait()
    stores = [
        pltpu.make_async_copy(held.at[side, slot], out.at[side], sent.at[at, side])
        for at, (out, slot) in enumerate(zip(outs, slots))
        for side in range(2)
    ]
    stores.append(pltpu.make_async_copy(new_held, new_out, sent.at[len(offsets), 0]))
    for copy in stores:
        copy.start()
    for copy in stores:
        copy.wait()


def pick(own, table, keys, values, new_keys, new_values, offsets):
    return pl.pallas_call(
        functools.partial(pick_kernel, offsets),
        out_shape=[jax.ShapeDtypeStruct((2, PAGE, HD), keys.dtype)] * len(offsets)
        + [jax.ShapeDtypeStruct((2,) + new_keys.shape, new_keys.dtype)],
        in_specs=[SMEM, SMEM] + [ANY] * 4,
        out_specs=[ANY] * (len(offsets) + 1),
        scratch_shapes=[
            pltpu.VMEM((2,) + keys.shape, keys.dtype),
            pltpu.VMEM((2,) + new_keys.shape, new_keys.dtype),
            pltpu.SemaphoreType.DMA((4,)),
            pltpu.SemaphoreType.DMA((len(offsets) + 1, 2)),
        ],
        compiler_params=pltpu.CompilerParams(vmem_limit_bytes=PICK_VMEM),
        name="pick",
    )(own, table, keys, values, new_keys, new_values)


def pack_kernel(count, *refs):
    for at in range(count):
        refs[-1][at] = refs[at][...]


def pack(arrays, after):
    count = len(arrays)
    return pl.pallas_call(
        functools.partial(pack_kernel, count),
        out_shape=jax.ShapeDtypeStruct((count,) + arrays[0].shape, arrays[0].dtype),
        in_specs=[VMEM] * count + [ANY] * len(after),
        out_specs=VMEM,
        compiler_params=pltpu.CompilerParams(vmem_limit_bytes=VMEM_BYTES),
        name="pack",
    )(*arrays, *after)


def online(scores, values, old_max, old_totals, old_acc, shares=None):
    width = scores.shape[1] // HD
    peak = jnp.max(scores, axis=1, keepdims=True)
    new_max = jnp.broadcast_to(peak, (scores.shape[0], HD))
    if old_max is not None:
        new_max = jnp.maximum(old_max, new_max)
    weights = jnp.exp2((scores - jnp.concatenate([new_max] * width, 1)) * EXP2_SCALE)
    parts = [weights[:, part * HD : (part + 1) * HD] for part in range(width)]
    if shares is not None:
        each = width // len(shares)
        parts = [sum(parts[at * each + 1 : (at + 1) * each], parts[at * each]) for at in range(len(shares))]
        parts = parts[:1] + [part * share for part, share in zip(parts[1:], shares[1:])]
    totals = sum(parts[1:], parts[0])
    acc = jnp.dot(weights.astype(jnp.bfloat16), values, preferred_element_type=jnp.float32)
    if old_max is not None:
        rescale = jnp.exp2((old_max - new_max) * EXP2_SCALE)
        totals = old_totals * rescale + totals
        acc = old_acc * rescale + acc
    return new_max, totals, acc


def score(query, keys):
    return lax.dot_general(query, keys, ROW_BY_ROW, preferred_element_type=jnp.float32)


def list_pages(cuts, own, table_ref, list_ref):
    chip, core = own // CORES, own % CORES
    key_heads, depth = table_ref.shape[1:]
    seen = 0
    for wave in range(WAVES):

        def look(page, seen, wave=wave):
            slot = table_ref[chip // key_heads, chip % key_heads, page]
            device = jnp.maximum(slot, 0) // SLOTS_DEV
            offset = jnp.bitwise_xor(device // CORES, chip)
            inside = (slot >= 0) & (offset >= cuts[wave]) & (offset < cuts[wave + 1])

            @pl.when(inside)
            def _():
                list_ref[HEAD + seen] = (cuts[wave + 1] - 1 - offset) * 2 + jnp.bitwise_xor(device % CORES, core)

            return seen + inside.astype(jnp.int32)

        seen = lax.fori_loop(0, depth, look, seen)
        list_ref[wave] = seen
    early = list_ref[WAVES - 2]
    late = seen - early
    rest = early % BLOCK
    more = (rest + late + BLOCK - 1) // BLOCK > (late + BLOCK - 1) // BLOCK
    list_ref[WAVES] = jnp.where(more, early, early - rest)


def stretch_kernel(cuts, own_ref, table_ref, q_ref, own_kv_ref, other_kv_ref, m_ref, l_ref, a_ref, done_ref, list_ref, ks, vs):
    list_pages(cuts, own_ref[0], table_ref, list_ref)
    half = own_ref[0] % CORES
    rows = own_kv_ref.shape[1]
    for place, source in ((half, own_kv_ref), (1 - half, other_kv_ref)):
        for side, target in enumerate((ks, vs)):
            target[pl.ds(pl.multiple_of(place * rows, rows), rows)] = source[side]
    done_ref[...] = jnp.zeros_like(done_ref)

    tiles = STRETCH // TILE
    row = lax.broadcasted_iota(jnp.int32, (TILE, TILE), 0)
    column = lax.broadcasted_iota(jnp.int32, (TILE, TILE), 1)

    def head(h, _):
        columns = pl.ds(pl.multiple_of(h * HD, HD), HD)

        def scores_of(tile):
            here = slice(tile * TILE, (tile + 1) * TILE)
            scores = score(q_ref[here, columns], ks[: (tile + 1) * TILE])
            last = jnp.where(column <= row, scores[:, tile * TILE :], -jnp.inf)
            if tile == 0:
                return last
            return jnp.concatenate([scores[:, : tile * TILE], last], 1)

        ahead = scores_of(tiles - 1)
        for tile in range(tiles)[::-1]:
            scores = ahead
            if tile > 0:
                ahead = scores_of(tile - 1)
            here = slice(tile * TILE, (tile + 1) * TILE)
            m, l, a = online(scores, vs[: (tile + 1) * TILE], None, None, None)
            m_ref[h, here, :] = m
            l_ref[h, here, :] = l
            a_ref[h, here, :] = a
        return 0

    lax.fori_loop(0, q_ref.shape[1] // HD, head, 0)


def pages_kernel(final, list_ref, q_ref, *refs):
    waves = WAVES if final else WAVES - 1
    sources = [(refs[2 * wave], refs[2 * wave + 1]) for wave in range(waves)]
    refs = refs[2 * waves :]
    if final:
        m_ref, l_ref, a_ref, o_ref, ks, vs, ahead_ref, held, sem = refs
    else:
        m_ref, l_ref, a_ref, done_ref, ks, vs, ahead_ref = refs[3:]
        done_ref[...] = jnp.zeros_like(done_ref)
    skipped = list_ref[WAVES] if final else 0
    limit = list_ref[WAVES - 1] if final else list_ref[WAVES]
    for wave, (near_ref, far_ref) in enumerate(sources):
        start = jnp.maximum(list_ref[wave - 1], skipped) if wave > 0 else skipped
        stop = jnp.minimum(list_ref[wave], limit)

        def take(at, _, near_ref=near_ref, far_ref=far_ref):
            place = list_ref[HEAD + at]
            there = place // 2

            @pl.when(place % 2 == 0)
            def _():
                ks[at - skipped] = near_ref[there, 0]
                vs[at - skipped] = near_ref[there, 1]

            @pl.when(place % 2 == 1)
            def _():
                ks[at - skipped] = far_ref[there, 0]
                vs[at - skipped] = far_ref[there, 1]

            return 0

        lax.fori_loop(start, stop, take, 0)

    filled = limit - skipped
    blocks = (filled + BLOCK - 1) // BLOCK

    def blank(at, _):
        ks[at] = ks[at // BLOCK * BLOCK]
        vs[at] = jnp.zeros((PAGE, HD), vs.dtype)
        return 0

    lax.fori_loop(filled, blocks * BLOCK, blank, 0)
    heads = q_ref.shape[1] // HD
    tiles = STRETCH // TILE
    rows = BLOCK * PAGE
    units = [(h, tile) for h in range(heads) for tile in range(tiles)]

    def scores_of(first, h, tile):
        keys = ks[pl.ds(first, BLOCK)].reshape(rows, HD)
        queries = q_ref[tile * TILE : (tile + 1) * TILE, h * HD : (h + 1) * HD]
        return score(queries, keys)

    @pl.when(blocks > 0)
    def _():
        ahead_ref[...] = scores_of(0, 0, 0)

    def block(at, _):
        first = at * BLOCK
        ahead = ahead_ref[...]
        shares = [jnp.where(first + page < filled, 1.0, 0.0) for page in range(BLOCK)]
        for unit, (h, tile) in enumerate(units):
            scores = ahead
            if unit + 1 < len(units):
                ahead = scores_of(first, *units[unit + 1])
            else:
                ahead_ref[...] = scores_of(jnp.minimum(at + 1, blocks - 1) * BLOCK, 0, 0)
            values = vs[pl.ds(first, BLOCK)].reshape(rows, HD)
            here = slice(tile * TILE, (tile + 1) * TILE)
            m, l, a = online(scores, values, m_ref[h, here, :], l_ref[h, here, :], a_ref[h, here, :], shares)
            m_ref[h, here, :] = m
            l_ref[h, here, :] = l
            a_ref[h, here, :] = a
        return 0

    lax.fori_loop(0, blocks, block, 0)

    if final:

        def out(h):
            columns = pl.ds(pl.multiple_of(h * HD, HD), HD)
            return pltpu.make_async_copy(held.at[h], o_ref.at[:, columns], sem.at[h])

        def finish(h, _):
            high = l_ref[h].astype(jnp.bfloat16)
            low = (l_ref[h] - high.astype(jnp.float32)).astype(jnp.bfloat16)
            ones = jnp.ones((2 * HD, HD), jnp.bfloat16)
            totals = jnp.dot(jnp.concatenate([high, low], 1), ones, preferred_element_type=jnp.float32)
            held[h] = (a_ref[h] / totals).astype(o_ref.dtype)
            out(h).start()
            return 0

        def leave(h, _):
            out(h).wait()
            return 0

        lax.fori_loop(0, heads, finish, 0)
        lax.fori_loop(0, heads, leave, 0)


COST = pl.CostEstimate(flops=1000, bytes_accessed=1000, transcendentals=0)


def attend_pages(cuts, final, pages, queries, received, state):
    waves = WAVES if final else WAVES - 1
    most = CORES * cuts[WAVES - 1]
    if final:
        most = BLOCK - 1 + CORES * (cuts[WAVES] - cuts[WAVES - 1])
    most = min(pages.shape[0] - HEAD, most)
    most = -(-most // BLOCK) * BLOCK
    s_shape = jax.ShapeDtypeStruct(state[0].shape, jnp.float32)
    at = 2 + 2 * waves
    heads = state[0].shape[0]
    return pl.pallas_call(
        functools.partial(pages_kernel, final),
        out_shape=jax.ShapeDtypeStruct(queries.shape, queries.dtype) if final else [s_shape] * 3 + [DONE],
        in_specs=[SMEM] + [VMEM] * (4 + 2 * waves),
        out_specs=ANY if final else [VMEM] * 4,
        input_output_aliases={} if final else {at: 0, at + 1: 1, at + 2: 2},
        scratch_shapes=[
            pltpu.VMEM((most, PAGE, HD), jnp.bfloat16),
            pltpu.VMEM((most, PAGE, HD), jnp.bfloat16),
            pltpu.VMEM((TILE, BLOCK * PAGE), jnp.float32),
        ]
        + final * [pltpu.VMEM((heads, STRETCH, HD), queries.dtype), pltpu.SemaphoreType.DMA((heads,))],
        compiler_params=pltpu.CompilerParams(vmem_limit_bytes=VMEM_BYTES),
        cost_estimate=COST,
        name="pages",
    )(pages, queries, *received, *state[:3])


def shards(queries, stretch_keys, stretch_values, pool_keys, pool_values, page_counts, page_table):
    own_index = lax.axis_index("pool")
    heads = queries.shape[1] // HD
    chips = lax.axis_size("pool") // CORES
    own = own_index.astype(jnp.int32).reshape(1)
    cuts = (0, chips * 3 // 4, chips)
    order = list(range(chips // 2, chips)) + list(range(1, chips // 2)) + [0]
    *pages, stretch = pick(own, page_table, pool_keys, pool_values, stretch_keys, stretch_values, order)
    picked = dict(zip(order, pages))
    got = {at: picked[at] if at == 0 else swapped(picked[at], "pool", at * CORES) for at in order}

    other_stretch = swapped(stretch, "pool", 1)
    s_shape = jax.ShapeDtypeStruct((heads, STRETCH, HD), jnp.float32)
    *state, pages = pl.pallas_call(
        functools.partial(stretch_kernel, cuts),
        out_shape=[s_shape] * 3 + [DONE, jax.ShapeDtypeStruct((HEAD + page_table.shape[2],), jnp.int32)],
        in_specs=[SMEM, SMEM] + [VMEM] * 3,
        out_specs=[VMEM] * 4 + [SMEM],
        scratch_shapes=[
            pltpu.VMEM((STRETCH, HD), jnp.bfloat16),
            pltpu.VMEM((STRETCH, HD), jnp.bfloat16),
        ],
        compiler_params=pltpu.CompilerParams(vmem_limit_bytes=VMEM_BYTES),
        cost_estimate=COST,
        name="stretch",
    )(own, page_table, queries, stretch, other_stretch)

    received = []
    after = state[3:]
    for wave in range(WAVES):
        mine = pack([got[at] for at in range(cuts[wave], cuts[wave + 1])[::-1]], after)
        received += [mine, swapped(mine, "pool", 1)]
        after = [mine]
        if wave >= WAVES - 2:
            state = attend_pages(cuts, wave == WAVES - 1, pages, queries, received, state)
            after = state[3:]
    return state


def solution(mesh):
    placed = (
        P(None, ("groups", "pool")),
        P(("groups", "pool"), None),
        P(("groups", "pool"), None),
        P(("groups", "pool"), None, None),
        P(("groups", "pool"), None, None),
        P("groups"),
        P("groups", None, None),
    )
    return jax.shard_map(
        shards, mesh=mesh, in_specs=placed, out_specs=P(None, ("groups", "pool")), check_vma=False
    )
```

```python
import functools
import math

import jax
import jax.numpy as jnp
from jax import lax
from jax.experimental import pallas as pl
from jax.experimental.pallas import tpu as pltpu
from jax.sharding import PartitionSpec as P

HD = 128
QH = 32
KVH = 4
PAGE = 256
STRETCH = 1024
SLOTS_DEV = 3
CORES = 2
TILE = 256
VMEM_BYTES = 24 * 2**20
PICK_VMEM = 56 * 2**20
BLOCK = 4
WAVES = 2
HEAD = WAVES + 1
EXP2_SCALE = math.log2(math.e) / math.sqrt(HD)
ROW_BY_ROW = (((1,), (1,)), ((), ()))

VMEM = pl.BlockSpec(memory_space=pltpu.VMEM)
SMEM = pl.BlockSpec(memory_space=pltpu.SMEM)
ANY = pl.BlockSpec(memory_space=pl.ANY)
DONE = jax.ShapeDtypeStruct((8, HD), jnp.float32)


def swapped(value, axis, mask):
    pairs = [(source, source ^ mask) for source in range(lax.axis_size(axis))]
    return lax.ppermute(value, axis, pairs)


def pick_kernel(offsets, own_ref, table_ref, keys_ref, values_ref, new_keys_ref, new_values_ref, *refs):
    *outs, new_out, held, new_held, sem, sent = refs
    loads = [
        pltpu.make_async_copy(source, held.at[side], sem.at[side])
        for side, source in enumerate((keys_ref, values_ref))
    ]
    loads += [
        pltpu.make_async_copy(source, new_held.at[side], sem.at[2 + side])
        for side, source in enumerate((new_keys_ref, new_values_ref))
    ]
    for copy in loads:
        copy.start()
    own = own_ref[0]
    first = own * SLOTS_DEV
    key_heads, depth = table_ref.shape[1:]
    slots = []
    for offset in offsets:
        row = jnp.bitwise_xor(own // CORES, offset)

        def look(page, slot, row=row):
            there = table_ref[row // key_heads, row % key_heads, page] - first
            return jnp.where((there >= 0) & (there < SLOTS_DEV), there, slot)

        slots.append(lax.fori_loop(0, depth, look, 0, unroll=True))
    for copy in loads:
        copy.wait()
    stores = [
        pltpu.make_async_copy(held.at[side, slot], out.at[side], sent.at[at, side])
        for at, (out, slot) in enumerate(zip(outs, slots))
        for side in range(2)
    ]
    stores.append(pltpu.make_async_copy(new_held, new_out, sent.at[len(offsets), 0]))
    for copy in stores:
        copy.start()
    for copy in stores:
        copy.wait()


def pick(own, table, keys, values, new_keys, new_values, offsets):
    return pl.pallas_call(
        functools.partial(pick_kernel, offsets),
        out_shape=[jax.ShapeDtypeStruct((2, PAGE, HD), keys.dtype)] * len(offsets)
        + [jax.ShapeDtypeStruct((2,) + new_keys.shape, new_keys.dtype)],
        in_specs=[SMEM, SMEM] + [ANY] * 4,
        out_specs=[ANY] * (len(offsets) + 1),
        scratch_shapes=[
            pltpu.VMEM((2,) + keys.shape, keys.dtype),
            pltpu.VMEM((2,) + new_keys.shape, new_keys.dtype),
            pltpu.SemaphoreType.DMA((4,)),
            pltpu.SemaphoreType.DMA((len(offsets) + 1, 2)),
        ],
        compiler_params=pltpu.CompilerParams(vmem_limit_bytes=PICK_VMEM),
        name="pick",
    )(own, table, keys, values, new_keys, new_values)


def pack_kernel(count, *refs):
    for at in range(count):
        refs[-1][at] = refs[at][...]


def pack(arrays, after):
    count = len(arrays)
    return pl.pallas_call(
        functools.partial(pack_kernel, count),
        out_shape=jax.ShapeDtypeStruct((count,) + arrays[0].shape, arrays[0].dtype),
        in_specs=[VMEM] * count + [ANY] * len(after),
        out_specs=VMEM,
        compiler_params=pltpu.CompilerParams(vmem_limit_bytes=VMEM_BYTES),
        name="pack",
    )(*arrays, *after)


def online(scores, values, old_max, old_totals, old_acc, shares=None):
    width = scores.shape[1] // HD
    peak = jnp.max(scores, axis=1, keepdims=True)
    new_max = jnp.broadcast_to(peak, (scores.shape[0], HD))
    if old_max is not None:
        new_max = jnp.maximum(old_max, new_max)
    weights = jnp.exp2((scores - jnp.concatenate([new_max] * width, 1)) * EXP2_SCALE)
    parts = [weights[:, part * HD : (part + 1) * HD] for part in range(width)]
    if shares is not None:
        each = width // len(shares)
        parts = [sum(parts[at * each + 1 : (at + 1) * each], parts[at * each]) for at in range(len(shares))]
        parts = parts[:1] + [part * share for part, share in zip(parts[1:], shares[1:])]
    totals = sum(parts[1:], parts[0])
    acc = jnp.dot(weights.astype(jnp.bfloat16), values, preferred_element_type=jnp.float32)
    if old_max is not None:
        rescale = jnp.exp2((old_max - new_max) * EXP2_SCALE)
        totals = old_totals * rescale + totals
        acc = old_acc * rescale + acc
    return new_max, totals, acc


def score(query, keys):
    return lax.dot_general(query, keys, ROW_BY_ROW, preferred_element_type=jnp.float32)


def list_pages(cuts, own, table_ref, list_ref):
    chip, core = own // CORES, own % CORES
    key_heads, depth = table_ref.shape[1:]
    seen = 0
    for wave in range(WAVES):

        def look(page, seen, wave=wave):
            slot = table_ref[chip // key_heads, chip % key_heads, page]
            device = jnp.maximum(slot, 0) // SLOTS_DEV
            offset = jnp.bitwise_xor(device // CORES, chip)
            inside = (slot >= 0) & (offset >= cuts[wave]) & (offset < cuts[wave + 1])

            place = (cuts[wave + 1] - 1 - offset) * 2 + jnp.bitwise_xor(device % CORES, core)
            list_ref[HEAD + jnp.where(inside, seen, depth)] = place
            return seen + inside.astype(jnp.int32)

        seen = lax.fori_loop(0, depth, look, seen, unroll=True)
        list_ref[wave] = seen
    early = list_ref[WAVES - 2]
    late = seen - early
    rest = early % BLOCK
    more = (rest + late + BLOCK - 1) // BLOCK > (late + BLOCK - 1) // BLOCK
    list_ref[WAVES] = jnp.where(more, early, early - rest)


def stretch_kernel(cuts, own_ref, table_ref, q_ref, own_kv_ref, other_kv_ref, page_ref, *refs):
    m_ref, l_ref, a_ref, done_ref, page_out_ref, list_ref, ks, vs = refs
    page_out_ref[...] = page_ref[...]
    list_pages(cuts, own_ref[0], table_ref, list_ref)
    half = own_ref[0] % CORES
    rows = own_kv_ref.shape[1]
    for place, source in ((half, own_kv_ref), (1 - half, other_kv_ref)):
        for side, target in enumerate((ks, vs)):
            target[pl.ds(pl.multiple_of(place * rows, rows), rows)] = source[side]
    done_ref[...] = jnp.zeros_like(done_ref)

    tiles = STRETCH // TILE
    row = lax.broadcasted_iota(jnp.int32, (TILE, TILE), 0)
    column = lax.broadcasted_iota(jnp.int32, (TILE, TILE), 1)

    def head(h, _):
        columns = pl.ds(pl.multiple_of(h * HD, HD), HD)

        def scores_of(tile):
            here = slice(tile * TILE, (tile + 1) * TILE)
            scores = score(q_ref[here, columns], ks[: (tile + 1) * TILE])
            last = jnp.where(column <= row, scores[:, tile * TILE :], -jnp.inf)
            if tile == 0:
                return last
            return jnp.concatenate([scores[:, : tile * TILE], last], 1)

        ahead = scores_of(tiles - 1)
        for tile in range(tiles)[::-1]:
            scores = ahead
            if tile > 0:
                ahead = scores_of(tile - 1)
            here = slice(tile * TILE, (tile + 1) * TILE)
            m, l, a = online(scores, vs[: (tile + 1) * TILE], None, None, None)
            m_ref[h, here, :] = m
            l_ref[h, here, :] = l
            a_ref[h, here, :] = a
        return 0

    lax.fori_loop(0, q_ref.shape[1] // HD, head, 0)


def pages_kernel(final, list_ref, q_ref, *refs):
    waves = WAVES if final else WAVES - 1
    sources = [(refs[2 * wave], refs[2 * wave + 1]) for wave in range(waves)]
    refs = refs[2 * waves :]
    if final:
        m_ref, l_ref, a_ref, o_ref, ks, vs, ahead_ref, held, sem = refs
    else:
        m_ref, l_ref, a_ref, done_ref, ks, vs, ahead_ref = refs[3:]
        done_ref[...] = jnp.zeros_like(done_ref)
    skipped = list_ref[WAVES] if final else 0
    limit = list_ref[WAVES - 1] if final else list_ref[WAVES]
    for wave, (near_ref, far_ref) in enumerate(sources):
        start = jnp.maximum(list_ref[wave - 1], skipped) if wave > 0 else skipped
        stop = jnp.minimum(list_ref[wave], limit)

        def take(at, _, near_ref=near_ref, far_ref=far_ref):
            place = list_ref[HEAD + at]
            there = place // 2

            @pl.when(place % 2 == 0)
            def _():
                ks[at - skipped] = near_ref[there, 0]
                vs[at - skipped] = near_ref[there, 1]

            @pl.when(place % 2 == 1)
            def _():
                ks[at - skipped] = far_ref[there, 0]
                vs[at - skipped] = far_ref[there, 1]

            return 0

        lax.fori_loop(start, stop, take, 0)

    filled = limit - skipped
    blocks = (filled + BLOCK - 1) // BLOCK

    def blank(at, _):
        ks[at] = ks[at // BLOCK * BLOCK]
        vs[at] = jnp.zeros((PAGE, HD), vs.dtype)
        return 0

    lax.fori_loop(filled, blocks * BLOCK, blank, 0)
    heads = q_ref.shape[1] // HD
    tiles = STRETCH // TILE
    rows = BLOCK * PAGE
    units = [(h, tile) for h in range(heads) for tile in range(tiles)]

    def scores_of(first, h, tile):
        keys = ks[pl.ds(first, BLOCK)].reshape(rows, HD)
        queries = q_ref[tile * TILE : (tile + 1) * TILE, h * HD : (h + 1) * HD]
        return score(queries, keys)

    @pl.when(blocks > 0)
    def _():
        ahead_ref[...] = scores_of(0, 0, 0)

    def block(at, _):
        first = at * BLOCK
        ahead = ahead_ref[...]
        shares = [jnp.where(first + page < filled, 1.0, 0.0) for page in range(BLOCK)]
        for unit, (h, tile) in enumerate(units):
            scores = ahead
            if unit + 1 < len(units):
                ahead = scores_of(first, *units[unit + 1])
            else:
                ahead_ref[...] = scores_of(jnp.minimum(at + 1, blocks - 1) * BLOCK, 0, 0)
            values = vs[pl.ds(first, BLOCK)].reshape(rows, HD)
            here = slice(tile * TILE, (tile + 1) * TILE)
            m, l, a = online(scores, values, m_ref[h, here, :], l_ref[h, here, :], a_ref[h, here, :], shares)
            m_ref[h, here, :] = m
            l_ref[h, here, :] = l
            a_ref[h, here, :] = a
        return 0

    lax.fori_loop(0, blocks, block, 0)

    if final:

        def out(h):
            columns = pl.ds(pl.multiple_of(h * HD, HD), HD)
            return pltpu.make_async_copy(held.at[h], o_ref.at[:, columns], sem.at[h])

        def finish(h, _):
            high = l_ref[h].astype(jnp.bfloat16)
            low = (l_ref[h] - high.astype(jnp.float32)).astype(jnp.bfloat16)
            ones = jnp.ones((2 * HD, HD), jnp.bfloat16)
            totals = jnp.dot(jnp.concatenate([high, low], 1), ones, preferred_element_type=jnp.float32)
            held[h] = (a_ref[h] / totals).astype(o_ref.dtype)
            out(h).start()
            return 0

        def leave(h, _):
            out(h).wait()
            return 0

        lax.fori_loop(0, heads, finish, 0)
        lax.fori_loop(0, heads, leave, 0)


COST = pl.CostEstimate(flops=1000, bytes_accessed=1000, transcendentals=0)


def attend_pages(cuts, final, pages, queries, received, state):
    waves = WAVES if final else WAVES - 1
    most = CORES * cuts[WAVES - 1]
    if final:
        most = BLOCK - 1 + CORES * (cuts[WAVES] - cuts[WAVES - 1])
    most = min(pages.shape[0] - HEAD - 1, most)
    most = -(-most // BLOCK) * BLOCK
    s_shape = jax.ShapeDtypeStruct(state[0].shape, jnp.float32)
    at = 2 + 2 * waves
    heads = state[0].shape[0]
    return pl.pallas_call(
        functools.partial(pages_kernel, final),
        out_shape=jax.ShapeDtypeStruct(queries.shape, queries.dtype) if final else [s_shape] * 3 + [DONE],
        in_specs=[SMEM] + [VMEM] * (4 + 2 * waves),
        out_specs=ANY if final else [VMEM] * 4,
        input_output_aliases={} if final else {at: 0, at + 1: 1, at + 2: 2},
        scratch_shapes=[
            pltpu.VMEM((most, PAGE, HD), jnp.bfloat16),
            pltpu.VMEM((most, PAGE, HD), jnp.bfloat16),
            pltpu.VMEM((TILE, BLOCK * PAGE), jnp.float32),
        ]
        + final * [pltpu.VMEM((heads, STRETCH, HD), queries.dtype), pltpu.SemaphoreType.DMA((heads,))],
        compiler_params=pltpu.CompilerParams(vmem_limit_bytes=VMEM_BYTES),
        cost_estimate=COST,
        name="pages",
    )(pages, queries, *received, *state[:3])


def shards(queries, stretch_keys, stretch_values, pool_keys, pool_values, page_counts, page_table):
    own_index = lax.axis_index("pool")
    heads = queries.shape[1] // HD
    chips = lax.axis_size("pool") // CORES
    own = own_index.astype(jnp.int32).reshape(1)
    cuts = (0, chips * 3 // 4, chips)
    order = list(range(chips // 2, chips)) + list(range(1, chips // 2)) + [0]
    *pages, stretch = pick(own, page_table, pool_keys, pool_values, stretch_keys, stretch_values, order)
    picked = dict(zip(order, pages))
    got = {at: picked[at] if at == 0 else swapped(picked[at], "pool", at * CORES) for at in order}

    other_stretch = swapped(stretch, "pool", 1)
    s_shape = jax.ShapeDtypeStruct((heads, STRETCH, HD), jnp.float32)
    *state, got[0], pages = pl.pallas_call(
        functools.partial(stretch_kernel, cuts),
        out_shape=[s_shape] * 3
        + [
            DONE,
            jax.ShapeDtypeStruct(got[0].shape, got[0].dtype),
            jax.ShapeDtypeStruct((HEAD + page_table.shape[2] + 1,), jnp.int32),
        ],
        in_specs=[SMEM, SMEM] + [VMEM] * 4,
        out_specs=[VMEM] * 5 + [SMEM],
        scratch_shapes=[
            pltpu.VMEM((STRETCH, HD), jnp.bfloat16),
            pltpu.VMEM((STRETCH, HD), jnp.bfloat16),
        ],
        compiler_params=pltpu.CompilerParams(vmem_limit_bytes=VMEM_BYTES),
        cost_estimate=COST,
        name="stretch",
    )(own, page_table, queries, stretch, other_stretch, got[0])

    received = []
    after = state[3:]
    for wave in range(WAVES):
        mine = pack([got[at] for at in range(cuts[wave], cuts[wave + 1])[::-1]], after)
        received += [mine, swapped(mine, "pool", 1)]
        after = [mine]
        if wave >= WAVES - 2:
            state = attend_pages(cuts, wave == WAVES - 1, pages, queries, received, state)
            after = state[3:]
    return state


def solution(mesh):
    placed = (
        P(None, ("groups", "pool")),
        P(("groups", "pool"), None),
        P(("groups", "pool"), None),
        P(("groups", "pool"), None, None),
        P(("groups", "pool"), None, None),
        P("groups"),
        P("groups", None, None),
    )
    return jax.shard_map(
        shards, mesh=mesh, in_specs=placed, out_specs=P(None, ("groups", "pool")), check_vma=False
    )
```

```python
import functools
import math

import jax
import jax.numpy as jnp
from jax import lax
from jax.experimental import pallas as pl
from jax.experimental.pallas import tpu as pltpu
from jax.sharding import PartitionSpec as P

HD = 128
QH = 32
KVH = 4
PAGE = 256
STRETCH = 1024
SLOTS_DEV = 3
CORES = 2
TILE = 256
VMEM_BYTES = 24 * 2**20
PICK_VMEM = 56 * 2**20
BLOCK = 4
WAVES = 2
HEAD = WAVES + 1
EXP2_SCALE = math.log2(math.e) / math.sqrt(HD)
ROW_BY_ROW = (((1,), (1,)), ((), ()))

VMEM = pl.BlockSpec(memory_space=pltpu.VMEM)
SMEM = pl.BlockSpec(memory_space=pltpu.SMEM)
ANY = pl.BlockSpec(memory_space=pl.ANY)
DONE = jax.ShapeDtypeStruct((8, HD), jnp.float32)


def swapped(value, axis, mask):
    pairs = [(source, source ^ mask) for source in range(lax.axis_size(axis))]
    return lax.ppermute(value, axis, pairs)


def pick_kernel(offsets, own_ref, table_ref, keys_ref, values_ref, new_keys_ref, new_values_ref, *refs):
    *outs, new_out, held, new_held, sem, sent = refs
    loads = [
        pltpu.make_async_copy(source, held.at[side], sem.at[side])
        for side, source in enumerate((keys_ref, values_ref))
    ]
    loads += [
        pltpu.make_async_copy(source, new_held.at[side], sem.at[2 + side])
        for side, source in enumerate((new_keys_ref, new_values_ref))
    ]
    for copy in loads:
        copy.start()
    own = own_ref[0]
    first = own * SLOTS_DEV
    key_heads, depth = table_ref.shape[1:]
    slots = []
    for offset in offsets:
        row = jnp.bitwise_xor(own // CORES, offset)

        def look(page, slot, row=row):
            there = table_ref[row // key_heads, row % key_heads, page] - first
            return jnp.where((there >= 0) & (there < SLOTS_DEV), there, slot)

        slots.append(lax.fori_loop(0, depth, look, 0, unroll=True))
    for copy in loads:
        copy.wait()
    rows = new_keys_ref.shape[0]
    targets = [[out.at[side] for side in range(2)] for out in outs]
    targets.append([new_out.at[side, pl.ds(rows, PAGE)] for side in range(2)])
    stores = [
        pltpu.make_async_copy(held.at[side, slot], target[side], sent.at[at, side])
        for at, (target, slot) in enumerate(zip(targets, slots))
        for side in range(2)
    ]
    stores += [
        pltpu.make_async_copy(new_held.at[side], new_out.at[side, pl.ds(0, rows)], sent.at[len(offsets), side])
        for side in range(2)
    ]
    for copy in stores:
        copy.start()
    for copy in stores:
        copy.wait()


def pick(own, table, keys, values, new_keys, new_values, offsets):
    return pl.pallas_call(
        functools.partial(pick_kernel, offsets),
        out_shape=[jax.ShapeDtypeStruct((2, PAGE, HD), keys.dtype)] * (len(offsets) - 1)
        + [jax.ShapeDtypeStruct((2, new_keys.shape[0] + PAGE, HD), new_keys.dtype)],
        in_specs=[SMEM, SMEM] + [ANY] * 4,
        out_specs=[ANY] * len(offsets),
        scratch_shapes=[
            pltpu.VMEM((2,) + keys.shape, keys.dtype),
            pltpu.VMEM((2,) + new_keys.shape, new_keys.dtype),
            pltpu.SemaphoreType.DMA((4,)),
            pltpu.SemaphoreType.DMA((len(offsets) + 1, 2)),
        ],
        compiler_params=pltpu.CompilerParams(vmem_limit_bytes=PICK_VMEM),
        name="pick",
    )(own, table, keys, values, new_keys, new_values)


def pack_kernel(count, *refs):
    for at in range(count):
        refs[-1][at] = refs[at][...]


def pack(arrays, after):
    count = len(arrays)
    return pl.pallas_call(
        functools.partial(pack_kernel, count),
        out_shape=jax.ShapeDtypeStruct((count,) + arrays[0].shape, arrays[0].dtype),
        in_specs=[VMEM] * count + [ANY] * len(after),
        out_specs=VMEM,
        compiler_params=pltpu.CompilerParams(vmem_limit_bytes=VMEM_BYTES),
        name="pack",
    )(*arrays, *after)


def online(scores, values, old_max, old_totals, old_acc, shares=None):
    width = scores.shape[1] // HD
    peak = jnp.max(scores, axis=1, keepdims=True)
    new_max = jnp.broadcast_to(peak, (scores.shape[0], HD))
    if old_max is not None:
        new_max = jnp.maximum(old_max, new_max)
    weights = jnp.exp2((scores - jnp.concatenate([new_max] * width, 1)) * EXP2_SCALE)
    parts = [weights[:, part * HD : (part + 1) * HD] for part in range(width)]
    if shares is not None:
        each = width // len(shares)
        parts = [sum(parts[at * each + 1 : (at + 1) * each], parts[at * each]) for at in range(len(shares))]
        parts = parts[:1] + [part * share for part, share in zip(parts[1:], shares[1:])]
    totals = sum(parts[1:], parts[0])
    acc = jnp.dot(weights.astype(jnp.bfloat16), values, preferred_element_type=jnp.float32)
    if old_max is not None:
        rescale = jnp.exp2((old_max - new_max) * EXP2_SCALE)
        totals = old_totals * rescale + totals
        acc = old_acc * rescale + acc
    return new_max, totals, acc


def score(query, keys):
    return lax.dot_general(query, keys, ROW_BY_ROW, preferred_element_type=jnp.float32)


def list_pages(cuts, own, table_ref, list_ref):
    chip, core = own // CORES, own % CORES
    key_heads, depth = table_ref.shape[1:]
    seen = 0
    for wave in range(WAVES):

        def look(page, seen, wave=wave):
            slot = table_ref[chip // key_heads, chip % key_heads, page]
            device = jnp.maximum(slot, 0) // SLOTS_DEV
            offset = jnp.bitwise_xor(device // CORES, chip)
            inside = (slot >= 0) & (offset >= cuts[wave]) & (offset < cuts[wave + 1])

            place = (cuts[wave + 1] - 1 - offset) * 2 + jnp.bitwise_xor(device % CORES, core)
            list_ref[HEAD + jnp.where(inside, seen, depth)] = place
            return seen + inside.astype(jnp.int32)

        seen = lax.fori_loop(0, depth, look, seen, unroll=True)
        list_ref[wave] = seen
    early = list_ref[WAVES - 2]
    late = seen - early
    rest = early % BLOCK
    more = (rest + late + BLOCK - 1) // BLOCK > (late + BLOCK - 1) // BLOCK
    list_ref[WAVES] = jnp.where(more, early, early - rest)


def stretch_kernel(cuts, own_ref, table_ref, q_ref, own_kv_ref, other_kv_ref, *refs):
    m_ref, l_ref, a_ref, done_ref, page_out_ref, list_ref, ks, vs = refs
    list_pages(cuts, own_ref[0], table_ref, list_ref)
    half = own_ref[0] % CORES
    rows = own_kv_ref.shape[1] - PAGE
    page_out_ref[...] = own_kv_ref[:, rows:]
    for place, source in ((half, own_kv_ref), (1 - half, other_kv_ref)):
        for side, target in enumerate((ks, vs)):
            target[pl.ds(pl.multiple_of(place * rows, rows), rows)] = source[side, :rows]
    done_ref[...] = jnp.zeros_like(done_ref)

    tiles = STRETCH // TILE
    row = lax.broadcasted_iota(jnp.int32, (TILE, TILE), 0)
    column = lax.broadcasted_iota(jnp.int32, (TILE, TILE), 1)

    def head(h, _):
        columns = pl.ds(pl.multiple_of(h * HD, HD), HD)

        def scores_of(tile):
            here = slice(tile * TILE, (tile + 1) * TILE)
            scores = score(q_ref[here, columns], ks[: (tile + 1) * TILE])
            last = jnp.where(column <= row, scores[:, tile * TILE :], -jnp.inf)
            if tile == 0:
                return last
            return jnp.concatenate([scores[:, : tile * TILE], last], 1)

        ahead = scores_of(tiles - 1)
        for tile in range(tiles)[::-1]:
            scores = ahead
            if tile > 0:
                ahead = scores_of(tile - 1)
            here = slice(tile * TILE, (tile + 1) * TILE)
            m, l, a = online(scores, vs[: (tile + 1) * TILE], None, None, None)
            m_ref[h, here, :] = m
            l_ref[h, here, :] = l
            a_ref[h, here, :] = a
        return 0

    lax.fori_loop(0, q_ref.shape[1] // HD, head, 0)


def pages_kernel(final, list_ref, q_ref, *refs):
    waves = WAVES if final else WAVES - 1
    sources = [(refs[2 * wave], refs[2 * wave + 1]) for wave in range(waves)]
    refs = refs[2 * waves :]
    if final:
        m_ref, l_ref, a_ref, o_ref, ks, vs, ahead_ref, held, sem = refs
    else:
        m_ref, l_ref, a_ref, done_ref, ks, vs, ahead_ref = refs[3:]
        done_ref[...] = jnp.zeros_like(done_ref)
    skipped = list_ref[WAVES] if final else 0
    limit = list_ref[WAVES - 1] if final else list_ref[WAVES]
    for wave, (near_ref, far_ref) in enumerate(sources):
        start = jnp.maximum(list_ref[wave - 1], skipped) if wave > 0 else skipped
        stop = jnp.minimum(list_ref[wave], limit)

        def take(at, _, near_ref=near_ref, far_ref=far_ref):
            place = list_ref[HEAD + at]
            there = place // 2

            @pl.when(place % 2 == 0)
            def _():
                ks[at - skipped] = near_ref[there, 0]
                vs[at - skipped] = near_ref[there, 1]

            @pl.when(place % 2 == 1)
            def _():
                ks[at - skipped] = far_ref[there, 0]
                vs[at - skipped] = far_ref[there, 1]

            return 0

        lax.fori_loop(start, stop, take, 0)

    filled = limit - skipped
    blocks = (filled + BLOCK - 1) // BLOCK

    def blank(at, _):
        ks[at] = ks[at // BLOCK * BLOCK]
        vs[at] = jnp.zeros((PAGE, HD), vs.dtype)
        return 0

    lax.fori_loop(filled, blocks * BLOCK, blank, 0)
    heads = q_ref.shape[1] // HD
    tiles = STRETCH // TILE
    rows = BLOCK * PAGE
    units = [(h, tile) for h in range(heads) for tile in range(tiles)]

    def scores_of(first, h, tile):
        keys = ks[pl.ds(first, BLOCK)].reshape(rows, HD)
        queries = q_ref[tile * TILE : (tile + 1) * TILE, h * HD : (h + 1) * HD]
        return score(queries, keys)

    @pl.when(blocks > 0)
    def _():
        ahead_ref[...] = scores_of(0, 0, 0)

    def block(at, _):
        first = at * BLOCK
        ahead = ahead_ref[...]
        shares = [jnp.where(first + page < filled, 1.0, 0.0) for page in range(BLOCK)]
        for unit, (h, tile) in enumerate(units):
            scores = ahead
            if unit + 1 < len(units):
                ahead = scores_of(first, *units[unit + 1])
            else:
                ahead_ref[...] = scores_of(jnp.minimum(at + 1, blocks - 1) * BLOCK, 0, 0)
            values = vs[pl.ds(first, BLOCK)].reshape(rows, HD)
            here = slice(tile * TILE, (tile + 1) * TILE)
            m, l, a = online(scores, values, m_ref[h, here, :], l_ref[h, here, :], a_ref[h, here, :], shares)
            m_ref[h, here, :] = m
            l_ref[h, here, :] = l
            a_ref[h, here, :] = a
        return 0

    lax.fori_loop(0, blocks, block, 0)

    if final:

        def out(h):
            columns = pl.ds(pl.multiple_of(h * HD, HD), HD)
            return pltpu.make_async_copy(held.at[h], o_ref.at[:, columns], sem.at[h])

        def finish(h, _):
            high = l_ref[h].astype(jnp.bfloat16)
            low = (l_ref[h] - high.astype(jnp.float32)).astype(jnp.bfloat16)
            ones = jnp.ones((2 * HD, HD), jnp.bfloat16)
            totals = jnp.dot(jnp.concatenate([high, low], 1), ones, preferred_element_type=jnp.float32)
            held[h] = (a_ref[h] / totals).astype(o_ref.dtype)
            out(h).start()
            return 0

        def leave(h, _):
            out(h).wait()
            return 0

        lax.fori_loop(0, heads, finish, 0)
        lax.fori_loop(0, heads, leave, 0)


COST = pl.CostEstimate(flops=1000, bytes_accessed=1000, transcendentals=0)


def attend_pages(cuts, final, pages, queries, received, state):
    waves = WAVES if final else WAVES - 1
    most = CORES * cuts[WAVES - 1]
    if final:
        most = BLOCK - 1 + CORES * (cuts[WAVES] - cuts[WAVES - 1])
    most = min(pages.shape[0] - HEAD - 1, most)
    most = -(-most // BLOCK) * BLOCK
    s_shape = jax.ShapeDtypeStruct(state[0].shape, jnp.float32)
    at = 2 + 2 * waves
    heads = state[0].shape[0]
    return pl.pallas_call(
        functools.partial(pages_kernel, final),
        out_shape=jax.ShapeDtypeStruct(queries.shape, queries.dtype) if final else [s_shape] * 3 + [DONE],
        in_specs=[SMEM] + [VMEM] * (4 + 2 * waves),
        out_specs=ANY if final else [VMEM] * 4,
        input_output_aliases={} if final else {at: 0, at + 1: 1, at + 2: 2},
        scratch_shapes=[
            pltpu.VMEM((most, PAGE, HD), jnp.bfloat16),
            pltpu.VMEM((most, PAGE, HD), jnp.bfloat16),
            pltpu.VMEM((TILE, BLOCK * PAGE), jnp.float32),
        ]
        + final * [pltpu.VMEM((heads, STRETCH, HD), queries.dtype), pltpu.SemaphoreType.DMA((heads,))],
        compiler_params=pltpu.CompilerParams(vmem_limit_bytes=VMEM_BYTES),
        cost_estimate=COST,
        name="pages",
    )(pages, queries, *received, *state[:3])


def shards(queries, stretch_keys, stretch_values, pool_keys, pool_values, page_counts, page_table):
    own_index = lax.axis_index("pool")
    heads = queries.shape[1] // HD
    chips = lax.axis_size("pool") // CORES
    own = own_index.astype(jnp.int32).reshape(1)
    cuts = (0, chips * 3 // 4, chips)
    order = list(range(chips // 2, chips)) + list(range(1, chips // 2)) + [0]
    *pages, stretch = pick(own, page_table, pool_keys, pool_values, stretch_keys, stretch_values, order)
    picked = dict(zip(order[:-1], pages))
    got = {at: swapped(picked[at], "pool", at * CORES) for at in order[:-1]}

    other_stretch = swapped(stretch, "pool", 1)
    s_shape = jax.ShapeDtypeStruct((heads, STRETCH, HD), jnp.float32)
    *state, got[0], pages = pl.pallas_call(
        functools.partial(stretch_kernel, cuts),
        out_shape=[s_shape] * 3
        + [
            DONE,
            jax.ShapeDtypeStruct((2, PAGE, HD), stretch.dtype),
            jax.ShapeDtypeStruct((HEAD + page_table.shape[2] + 1,), jnp.int32),
        ],
        in_specs=[SMEM, SMEM] + [VMEM] * 3,
        out_specs=[VMEM] * 5 + [SMEM],
        scratch_shapes=[
            pltpu.VMEM((STRETCH, HD), jnp.bfloat16),
            pltpu.VMEM((STRETCH, HD), jnp.bfloat16),
        ],
        compiler_params=pltpu.CompilerParams(vmem_limit_bytes=VMEM_BYTES),
        cost_estimate=COST,
        name="stretch",
    )(own, page_table, queries, stretch, other_stretch)

    received = []
    after = state[3:]
    for wave in range(WAVES):
        mine = pack([got[at] for at in range(cuts[wave], cuts[wave + 1])[::-1]], after)
        received += [mine, swapped(mine, "pool", 1)]
        after = [mine]
        if wave >= WAVES - 2:
            state = attend_pages(cuts, wave == WAVES - 1, pages, queries, received, state)
            after = state[3:]
    return state


def solution(mesh):
    placed = (
        P(None, ("groups", "pool")),
        P(("groups", "pool"), None),
        P(("groups", "pool"), None),
        P(("groups", "pool"), None, None),
        P(("groups", "pool"), None, None),
        P("groups"),
        P("groups", None, None),
    )
    return jax.shard_map(
        shards, mesh=mesh, in_specs=placed, out_specs=P(None, ("groups", "pool")), check_vma=False
    )
```
